512 devices in a mesh: mode: 32 (over y, x_hi, core), wave: 16 (over x_lo, z).
Axes of the slice: x: 4 (x_hi: 2, x_lo: 2; x = x_hi * 2 + x_lo), y: 8, z: 8, core: 2. Of those that a mesh axis runs over, the one named last changes fastest.
Arguments:
- field_in: bfloat16 [16, 32, 2, 512, 512], P('wave', 'mode'), may hold values from -6 to 6
- target: bfloat16 [16, 32, 2, 512, 512], P('wave', 'mode'), may hold values from -6 to 6
- mask_old: bfloat16 [2, 512, 512], replicated, may hold values from -1 to 1
- scales: float32 [16], P('wave'), may hold values from 0.5 to 2
Outputs:
- mask_one: bfloat16 [2, 512, 512], P(None, 'mode')
- mask_two: bfloat16 [2, 512, 512], P(None, 'mode')
The draws below stay inside these ranges and needn't reach their ends.
All inputs are finite; a program needn't handle non-finite values.
Results may differ from the reference program's by a relative error of at most 0.013.
Values may be sent and summed in bfloat16 or wider, within the bound.
No kernel may reach another device: no remote copies, remote signals or barrier semaphores. Data moves between devices by JAX's collectives and lax.ppermute only.
A program may use at most 64 MiB of HBM per device.

```python
import math
import jax
import jax.numpy as jnp
from jax import lax

PIXELS = 512
MODES = 32
WAVES = 16


def steps_of(own_key, extent, cuts, least, largest):
    def one(position, blocks):
        heights = jax.random.uniform(jax.random.fold_in(jax.random.fold_in(own_key, 6), position), (blocks,), jnp.float32, least / len(cuts), largest / len(cuts))
        return jnp.repeat(jnp.exp(heights), extent[position] // blocks).reshape((-1,) + (1,) * (len(extent) - position - 1))

    level = one(*cuts[0])
    for cut in cuts[1:]:
        level = level * one(*cut)
    return level


def noise(stream_key, shape, spread, bound, cuts=(), kind=jnp.bfloat16):
    entries = jax.random.normal(stream_key, shape, jnp.float32) * spread
    if len(cuts) > 0:
        entries = steps_of(stream_key, shape, cuts, -0.22, 0.18) * entries
    return jnp.clip(entries, min=-bound, max=bound).astype(kind)


def setup_inputs(seed: int = 0) -> dict:
    keys = jax.random.split(jax.random.key(seed), 5)
    return {
        "field_in": noise(keys[0], (WAVES, MODES, 2, PIXELS, PIXELS), 1.0, 6.0, ((0, 16), (1, 32))),
        "target": noise(keys[1], (WAVES, MODES, 2, PIXELS, PIXELS), 1.0, 6.0, ((0, 16), (1, 32))),
        "mask_old": jnp.clip(jax.random.uniform(keys[2], (2, PIXELS, PIXELS), jnp.float32, -1.0, 1.0), -1.0, 1.0).astype(jnp.bfloat16),
        "scales": jnp.clip(jnp.exp(math.log(2.0) - 1.3862944 * jax.random.uniform(keys[3], (WAVES,), jnp.float32) ** steps_of(keys[3], (WAVES,), ((0, 16),), -0.2, 0.2)), 0.5, 2.0),
    }


def chirp(scale, count):
    pos = jnp.arange(count, dtype=jnp.float32)
    diff = pos[:, None] - pos[None, :]
    angle = jnp.pi * scale * diff * diff / count
    factor = jnp.float32(count) ** (-0.5)
    return ((jnp.cos(angle) * factor).astype(jnp.bfloat16), (jnp.sin(angle) * factor).astype(jnp.bfloat16))

def right_matrix(real_part, imag_part, sign):
    upper = jnp.concatenate([real_part, sign * imag_part], 1)
    lower = jnp.concatenate([-sign * imag_part, real_part], 1)
    return jnp.concatenate([upper, lower], 0)

def left_matrix(real_part, imag_part, sign):
    first = jnp.concatenate([real_part, sign * imag_part], 0)
    second = jnp.concatenate([-sign * imag_part, real_part], 0)
    return jnp.stack([first, second], 0)

def propagate(field_re, field_im, real_part, imag_part, sign):
    count = field_re.shape[-1]
    batch = field_re.shape[0]
    joined = jnp.concatenate([field_re, field_im], -1).astype(jnp.float32)
    right = right_matrix(real_part, imag_part, sign).astype(jnp.float32)
    middle = jnp.einsum('brk,kc->brc', joined, right, precision=lax.Precision.HIGHEST).astype(jnp.bfloat16)
    middle = middle.reshape(batch, count, 2, count).astype(jnp.float32)
    left = left_matrix(real_part, imag_part, sign).astype(jnp.float32)
    result = jnp.einsum('pqk,bkpc->bqc', left, middle, precision=lax.Precision.HIGHEST)
    return (result[:, :count], result[:, count:])

def phasor(total):
    count = total.shape[-1] // 2
    power = jnp.sum(total * total) / (count * count)
    real_part = total[:, :count]
    imag_part = total[:, count:]
    factor = lax.rsqrt(real_part * real_part + imag_part * imag_part + power + 1e-06)
    return jnp.stack([real_part * factor, imag_part * factor], 0).astype(jnp.bfloat16)

def reference(field_in, target, mask_old, scales):
    old_re = mask_old[0].astype(jnp.float32)
    old_im = mask_old[1].astype(jnp.float32)

    def backward(carry, items):
        fields, targets, scale = items
        kernel_re, kernel_im = chirp(scale, PIXELS)
        f_re = fields[:, 0].astype(jnp.float32)
        f_im = fields[:, 1].astype(jnp.float32)
        b_re = targets[:, 0].astype(jnp.float32)
        b_im = targets[:, 1].astype(jnp.float32)
        c_re = (b_re * old_re + b_im * old_im).astype(jnp.bfloat16)
        c_im = (b_im * old_re - b_re * old_im).astype(jnp.bfloat16)
        back_re, back_im = propagate(c_re, c_im, kernel_re, kernel_im, -1.0)
        term = jnp.concatenate([lax.optimization_barrier(jnp.sum(back_re * f_re + back_im * f_im, 0)), lax.optimization_barrier(jnp.sum(back_im * f_re - back_re * f_im, 0))], -1)
        return (carry + term, None)
    start = jnp.zeros((PIXELS, 2 * PIXELS), jnp.float32)
    margin_one, unused = lax.scan(backward, start, (field_in, target, scales))
    mask_one = phasor(margin_one)
    new_re = mask_one[0].astype(jnp.float32)
    new_im = mask_one[1].astype(jnp.float32)

    def forward(carry, items):
        fields, targets, scale = items
        kernel_re, kernel_im = chirp(scale, PIXELS)
        f_re = fields[:, 0].astype(jnp.float32)
        f_im = fields[:, 1].astype(jnp.float32)
        b_re = targets[:, 0].astype(jnp.float32)
        b_im = targets[:, 1].astype(jnp.float32)
        g_re = (f_re * new_re - f_im * new_im).astype(jnp.bfloat16)
        g_im = (f_re * new_im + f_im * new_re).astype(jnp.bfloat16)
        ahead_re, ahead_im = propagate(g_re, g_im, kernel_re, kernel_im, 1.0)
        term = jnp.concatenate([lax.optimization_barrier(jnp.sum(b_re * ahead_re + b_im * ahead_im, 0)), lax.optimization_barrier(jnp.sum(b_im * ahead_re - b_re * ahead_im, 0))], -1)
        return (carry + term, None)
    margin_two, unused = lax.scan(forward, start, (field_in, target, scales))
    mask_two = phasor(margin_two)
    return (mask_one, mask_two)
```

```python
import jax
import jax.numpy as jnp
from jax import lax
from jax.experimental import pallas as pl
from jax.experimental.pallas import tpu as pltpu
from jax.sharding import Mesh, PartitionSpec as P

N = 512
BF = jnp.bfloat16
F32 = jnp.float32
AXES = ("y", "xh", "c", "xl", "z")
SIZES = (8, 2, 2, 2, 8)
MODE = ("y", "xh", "c")
WAVE = ("xl", "z")
VMEM_LIMIT = 40 * 1024 * 1024
BLK = 128


def dot(a, b):
    return jnp.dot(a, b, preferred_element_type=F32)


def chirp_into(scale, ar, ai):
    lane = lax.broadcasted_iota(jnp.int32, (8, 2 * N), 1)
    diff = (lane - N).astype(F32)
    angle = jnp.float32(jnp.pi) * scale * diff * diff / N
    factor = jnp.float32(N) ** (-0.5)
    for ref, fn in ((ar, jnp.cos), (ai, jnp.sin)):
        line = fn(angle) * factor
        for d in range(-3, 4):
            start = N + BLK * d - BLK
            window = line[0:1, start : start + 2 * BLK]
            window = jnp.broadcast_to(window, (BLK, 2 * BLK))
            rolled = pltpu.roll(window, BLK, 1, stride=1, stride_axis=0)
            block = rolled[:, :BLK].astype(BF)
            for row in range(4):
                col = row + d
                if 0 <= col < 4:
                    ref[row * BLK : (row + 1) * BLK, col * BLK : (col + 1) * BLK] = block


def back_kernel(scale_ref, core_ref, tgt_hbm, old_hbm, fld_hbm, ar, ai, keep, send, tgt, old, fld, z_s, sems):
    copies = [
        pltpu.make_async_copy(src, dst, sems.at[i])
        for i, (src, dst) in enumerate(((tgt_hbm, tgt), (old_hbm, old), (fld_hbm, fld)))
    ]
    for copy in copies:
        copy.start()
    chirp_into(scale_ref[0], ar, ai)
    copies[0].wait()
    copies[1].wait()
    for r in range(0, N, BLK):
        rows = slice(r, r + BLK)
        br = tgt[0, rows].astype(F32)
        bi = tgt[1, rows].astype(F32)
        mr = old[0, rows].astype(F32)
        mi = old[1, rows].astype(F32)
        cr = (br * mr + bi * mi).astype(BF)
        ci = (bi * mr - br * mi).astype(BF)
        z_s[0, rows] = (dot(cr, ar[...]) + dot(ci, ai[...])).astype(BF)
        z_s[1, rows] = (dot(ci, ar[...]) - dot(cr, ai[...])).astype(BF)
    copies[2].wait()
    first = core_ref[0] == 0
    for r in range(0, N, BLK):
        rows = slice(r, r + BLK)
        kr = ar[rows]
        ki = ai[rows]
        back_r = dot(kr, z_s[0]) + dot(ki, z_s[1])
        back_i = dot(kr, z_s[1]) - dot(ki, z_s[0])
        fr = fld[0, rows].astype(F32)
        fi = fld[1, rows].astype(F32)
        term_r = back_r * fr + back_i * fi
        term_i = back_i * fr - back_r * fi
        keep[rows] = jnp.where(first, term_r, term_i)
        send[rows] = jnp.where(first, term_i, term_r).astype(BF)


def ahead_kernel(core_ref, mode_ref, own, other, ar, ai, tgt_hbm, fld_hbm, mask_out, keep, send, tgt, fld, mask, z_s, sems):
    copies = [
        pltpu.make_async_copy(src, dst, sems.at[i])
        for i, (src, dst) in enumerate(((fld_hbm, fld), (tgt_hbm, tgt)))
    ]
    for copy in copies:
        copy.start()
    first = core_ref[0] == 0
    total = jnp.zeros((8, N), F32)
    for r in range(0, N, 8):
        a = own[r // 8].astype(F32)
        b = other[r // 8].astype(F32)
        total = total + (a * a + b * b)
    bias = jnp.sum(total) / (N * N) + 1e-06
    copies[0].wait()
    for r in range(0, N, BLK):
        rows = slice(r, r + BLK)
        a = own[r // 8 : (r + BLK) // 8].reshape(BLK, N).astype(F32)
        b = other[r // 8 : (r + BLK) // 8].reshape(BLK, N).astype(F32)
        factor = lax.rsqrt(a * a + b * b + bias)
        a = a * factor
        b = b * factor
        mr = jnp.where(first, a, b).astype(BF)
        mi = jnp.where(first, b, a).astype(BF)
        mask[0, rows] = mr
        mask[1, rows] = mi
        mr = mr.astype(F32)
        mi = mi.astype(F32)
        fr = fld[0, rows].astype(F32)
        fi = fld[1, rows].astype(F32)
        gr = (fr * mr - fi * mi).astype(BF)
        gi = (fr * mi + fi * mr).astype(BF)
        z_s[0, rows] = (dot(gr, ar[...]) - dot(gi, ai[...])).astype(BF)
        z_s[1, rows] = (dot(gi, ar[...]) + dot(gr, ai[...])).astype(BF)
    start = pl.multiple_of(mode_ref[0] * 16, 16)
    mask_out[0] = mask[0, pl.ds(start, 16)]
    mask_out[1] = mask[1, pl.ds(start, 16)]
    copies[1].wait()
    for r in range(0, N, BLK):
        rows = slice(r, r + BLK)
        kr = ar[rows]
        ki = ai[rows]
        ahead_r = dot(kr, z_s[0]) - dot(ki, z_s[1])
        ahead_i = dot(kr, z_s[1]) + dot(ki, z_s[0])
        br = tgt[0, rows].astype(F32)
        bi = tgt[1, rows].astype(F32)
        term_r = br * ahead_r + bi * ahead_i
        term_i = bi * ahead_r - br * ahead_i
        for q in range(BLK // 32):
            for part, term in ((0, term_r), (1, term_i)):
                even = term[q * 32 : q * 32 + 16]
                odd = term[q * 32 + 16 : q * 32 + 32]
                keep[r // 32 + q, part] = jnp.where(first, even, odd)
                send[r // 32 + q, part] = jnp.where(first, odd, even).astype(BF)


ANY = pl.BlockSpec(memory_space=pl.ANY)
SMEM = pl.BlockSpec(memory_space=pltpu.SMEM)
VMEM = pl.BlockSpec(memory_space=pltpu.VMEM)
PARAMS = pltpu.CompilerParams(vmem_limit_bytes=VMEM_LIMIT)


def call_back(scale, core, tgt, old, fld):
    return pl.pallas_call(
        back_kernel,
        out_shape=(
            jax.ShapeDtypeStruct((N, N), BF),
            jax.ShapeDtypeStruct((N, N), BF),
            jax.ShapeDtypeStruct((N, N), F32),
            jax.ShapeDtypeStruct((N, N), BF),
        ),
        in_specs=[SMEM, SMEM, ANY, ANY, ANY],
        out_specs=(VMEM,) * 4,
        scratch_shapes=[
            pltpu.VMEM((2, N, N), BF),
            pltpu.VMEM((2, N, N), BF),
            pltpu.VMEM((2, N, N), BF),
            pltpu.VMEM((2, N, N), BF),
            pltpu.SemaphoreType.DMA((3,)),
        ],
        compiler_params=PARAMS,
        name="back_margin",
    )(scale, core, tgt, old, fld)


def call_ahead(core, mode, own, other, ar, ai, tgt, fld):
    return pl.pallas_call(
        ahead_kernel,
        out_shape=(
            jax.ShapeDtypeStruct((2, 16, N), BF),
            jax.ShapeDtypeStruct((16, 2, 16, N), F32),
            jax.ShapeDtypeStruct((16, 2, 16, N), BF),
        ),
        in_specs=[SMEM, SMEM, VMEM, VMEM, VMEM, VMEM, ANY, ANY],
        out_specs=(VMEM,) * 3,
        scratch_shapes=[
            pltpu.VMEM((2, N, N), BF),
            pltpu.VMEM((2, N, N), BF),
            pltpu.VMEM((2, N, N), BF),
            pltpu.VMEM((2, N, N), BF),
            pltpu.SemaphoreType.DMA((2,)),
        ],
        compiler_params=PARAMS,
        name="ahead_margin",
    )(core, mode, own, other, ar, ai, tgt, fld)


def exchange(x, axes):
    return lax.all_to_all(x, axes, 0, 0, tiled=True)


def spread(x, axes, count):
    return exchange(jnp.broadcast_to(x[None], (count,) + x.shape), axes)


def total_of(x):
    return jnp.sum(x.astype(F32), 0)


def swap_cores(x):
    return lax.ppermute(x, "c", [(0, 1), (1, 0)])


def local(field_in, target, mask_old, scales):
    fld = field_in[0, 0]
    tgt = target[0, 0]
    core = lax.axis_index("c").reshape(1)
    mode = lax.axis_index(MODE).reshape(1)
    ar, ai, keep, send = call_back(scales, core, tgt, mask_old, fld)
    half = (keep + swap_cores(send).astype(F32)).astype(BF)
    part = total_of(exchange(half.reshape(64, 8, N), ("y", "z"))).astype(BF)
    part = total_of(spread(part, ("xh", "xl"), 4)).astype(BF)
    own = spread(part, ("y", "z"), 64)
    other = swap_cores(own)
    mask_one, keep, send = call_ahead(core, mode, own, other, ar, ai, tgt, fld)
    half = (keep + swap_cores(send).astype(F32)).astype(BF)
    part = total_of(exchange(half, ("y", "xh"))).astype(BF)
    rows = total_of(spread(part, WAVE, 16))
    power = jnp.sum(rows * rows)
    power = spread(jnp.broadcast_to(power.reshape(1, 1), (1, 128)), MODE, 32)
    power = jnp.sum(power[:, :, :1]) / (N * N)
    factor = lax.rsqrt(rows[0] * rows[0] + rows[1] * rows[1] + power + 1e-06)
    return mask_one, (rows * factor[None]).astype(BF)


def solution(mesh):
    fine = Mesh(mesh.devices.reshape(SIZES), AXES)
    data = P(WAVE, MODE, None, None, None)
    rows = P(None, MODE, None)
    return jax.shard_map(
        local,
        mesh=fine,
        in_specs=(data, data, P(), P(WAVE)),
        out_specs=(rows, rows),
        check_vma=False,
    )
```

```python
import jax
import jax.numpy as jnp
from jax import lax
from jax.experimental import pallas as pl
from jax.experimental.pallas import tpu as pltpu
from jax.sharding import Mesh, PartitionSpec as P

N = 512
BF = jnp.bfloat16
F32 = jnp.float32
AXES = ("y", "xh", "c", "xl", "z")
SIZES = (8, 2, 2, 2, 8)
MODE = ("y", "xh", "c")
WAVE = ("xl", "z")
MIB = 1024 * 1024
BLK = 128


def dot(a, b):
    return jnp.dot(a, b, preferred_element_type=F32)


def chirp_into(scale, ar, ai):
    lane = lax.broadcasted_iota(jnp.int32, (8, 2 * N), 1)
    diff = (lane - N).astype(F32)
    angle = jnp.float32(jnp.pi) * scale * diff * diff / N
    factor = jnp.float32(N) ** (-0.5)
    for ref, fn in ((ar, jnp.cos), (ai, jnp.sin)):
        line = fn(angle) * factor
        for d in range(-3, 4):
            start = N + BLK * d - BLK
            window = line[0:1, start : start + 2 * BLK]
            window = jnp.broadcast_to(window, (BLK, 2 * BLK))
            rolled = pltpu.roll(window, BLK, 1, stride=1, stride_axis=0)
            block = rolled[:, :BLK].astype(BF)
            for row in range(4):
                col = row + d
                if 0 <= col < 4:
                    ref[row * BLK : (row + 1) * BLK, col * BLK : (col + 1) * BLK] = block


def back_kernel(scale_ref, core_ref, tgt_hbm, old_hbm, fld_hbm, ar, ai, keep, send, tgt, old, fld, z_s, sems):
    copies = [
        pltpu.make_async_copy(src, dst, sems.at[i])
        for i, (src, dst) in enumerate(((tgt_hbm, tgt), (old_hbm, old), (fld_hbm, fld)))
    ]
    for copy in copies:
        copy.start()
    chirp_into(scale_ref[0], ar, ai)
    copies[0].wait()
    copies[1].wait()
    for r in range(0, N, BLK):
        rows = slice(r, r + BLK)
        br = tgt[0, rows].astype(F32)
        bi = tgt[1, rows].astype(F32)
        mr = old[0, rows].astype(F32)
        mi = old[1, rows].astype(F32)
        cr = (br * mr + bi * mi).astype(BF)
        ci = (bi * mr - br * mi).astype(BF)
        z_s[0, rows] = (dot(cr, ar[...]) + dot(ci, ai[...])).astype(BF)
        z_s[1, rows] = (dot(ci, ar[...]) - dot(cr, ai[...])).astype(BF)
    copies[2].wait()
    first = core_ref[0] == 0
    for r in range(0, N, BLK):
        rows = slice(r, r + BLK)
        kr = ar[rows]
        ki = ai[rows]
        back_r = dot(kr, z_s[0]) + dot(ki, z_s[1])
        back_i = dot(kr, z_s[1]) - dot(ki, z_s[0])
        fr = fld[0, rows].astype(F32)
        fi = fld[1, rows].astype(F32)
        term_r = back_r * fr + back_i * fi
        term_i = back_i * fr - back_r * fi
        keep[rows] = jnp.where(first, term_r, term_i)
        send[rows] = jnp.where(first, term_i, term_r).astype(BF)


def ahead_kernel(core_ref, mode_ref, own, other, ar, ai, tgt, fld, mask_out, keep, send, mask, z_s):
    first = core_ref[0] == 0
    total = jnp.zeros((32, N), F32)
    for r in range(16):
        a = own[r].astype(F32)
        b = other[r].astype(F32)
        total = total + (a * a + b * b)
    bias = jnp.sum(total) / (N * N) + 1e-06
    for r in range(0, N, BLK):
        rows = slice(r, r + BLK)
        a = own[r // 32 : (r + BLK) // 32].reshape(BLK, N).astype(F32)
        b = other[r // 32 : (r + BLK) // 32].reshape(BLK, N).astype(F32)
        factor = lax.rsqrt(a * a + b * b + bias)
        a = a * factor
        b = b * factor
        mr = jnp.where(first, a, b).astype(BF)
        mi = jnp.where(first, b, a).astype(BF)
        mask[0, rows] = mr
        mask[1, rows] = mi
        mr = mr.astype(F32)
        mi = mi.astype(F32)
        fr = fld[0, rows].astype(F32)
        fi = fld[1, rows].astype(F32)
        gr = (fr * mr - fi * mi).astype(BF)
        gi = (fr * mi + fi * mr).astype(BF)
        z_s[0, rows] = (dot(gr, ar[...]) - dot(gi, ai[...])).astype(BF)
        z_s[1, rows] = (dot(gi, ar[...]) + dot(gr, ai[...])).astype(BF)
    start = pl.multiple_of(mode_ref[0] * 16, 16)
    mask_out[0] = mask[0, pl.ds(start, 16)]
    mask_out[1] = mask[1, pl.ds(start, 16)]
    for r in range(0, N, BLK):
        rows = slice(r, r + BLK)
        kr = ar[rows]
        ki = ai[rows]
        ahead_r = dot(kr, z_s[0]) - dot(ki, z_s[1])
        ahead_i = dot(kr, z_s[1]) + dot(ki, z_s[0])
        br = tgt[0, rows].astype(F32)
        bi = tgt[1, rows].astype(F32)
        term_r = br * ahead_r + bi * ahead_i
        term_i = bi * ahead_r - br * ahead_i
        for q in range(BLK // 32):
            for part, term in ((0, term_r), (1, term_i)):
                even = term[q * 32 : q * 32 + 16]
                odd = term[q * 32 + 16 : q * 32 + 32]
                keep[r // 32 + q, part] = jnp.where(first, even, odd)
                send[r // 32 + q, part] = jnp.where(first, odd, even).astype(BF)


def power_kernel(parts, rows, power):
    total = parts[0].astype(F32)
    for w in range(1, 16):
        total = total + parts[w].astype(F32)
    rows[...] = total
    power[...] = jnp.broadcast_to(jnp.sum(total * total), (32, 1, 128))


def phasor_kernel(rows, power, out):
    total = power[0]
    for w in range(1, 32):
        total = total + power[w]
    bias = total[:, :1] / (N * N) + 1e-06
    a = rows[0]
    b = rows[1]
    factor = lax.rsqrt(a * a + b * b + bias)
    out[0] = (a * factor).astype(BF)
    out[1] = (b * factor).astype(BF)


HBM = pl.BlockSpec(memory_space=pltpu.HBM)
SMEM = pl.BlockSpec(memory_space=pltpu.SMEM)
VMEM = pl.BlockSpec(memory_space=pltpu.VMEM)


def call_back(scale, core, tgt, old, fld):
    return pl.pallas_call(
        back_kernel,
        out_shape=(
            jax.ShapeDtypeStruct((N, N), BF),
            jax.ShapeDtypeStruct((N, N), BF),
            jax.ShapeDtypeStruct((N, N), F32),
            jax.ShapeDtypeStruct((N, N), BF),
        ),
        in_specs=[SMEM, SMEM, HBM, HBM, HBM],
        out_specs=(VMEM,) * 4,
        scratch_shapes=[
            pltpu.VMEM((2, N, N), BF),
            pltpu.VMEM((2, N, N), BF),
            pltpu.VMEM((2, N, N), BF),
            pltpu.VMEM((2, N, N), BF),
            pltpu.SemaphoreType.DMA((3,)),
        ],
        compiler_params=pltpu.CompilerParams(vmem_limit_bytes=16 * MIB),
        name="back_margin",
    )(scale, core, tgt, old, fld)


def call_ahead(core, mode, own, other, ar, ai, tgt, fld):
    return pl.pallas_call(
        ahead_kernel,
        out_shape=(
            jax.ShapeDtypeStruct((2, 16, N), BF),
            jax.ShapeDtypeStruct((16, 2, 16, N), F32),
            jax.ShapeDtypeStruct((16, 2, 16, N), BF),
        ),
        in_specs=[SMEM, SMEM] + [VMEM] * 6,
        out_specs=(VMEM,) * 3,
        scratch_shapes=[pltpu.VMEM((2, N, N), BF), pltpu.VMEM((2, N, N), BF)],
        compiler_params=pltpu.CompilerParams(vmem_limit_bytes=16 * MIB),
        name="ahead_margin",
    )(core, mode, own, other, ar, ai, tgt, fld)


def call_power(parts):
    return pl.pallas_call(
        power_kernel,
        out_shape=(jax.ShapeDtypeStruct((2, 16, N), F32), jax.ShapeDtypeStruct((32, 1, 128), F32)),
        in_specs=[VMEM],
        out_specs=(VMEM, VMEM),
        compiler_params=pltpu.CompilerParams(vmem_limit_bytes=8 * MIB),
        name="row_power",
    )(parts)


def call_phasor(rows, power):
    return pl.pallas_call(
        phasor_kernel,
        out_shape=jax.ShapeDtypeStruct((2, 16, N), BF),
        in_specs=[VMEM, VMEM],
        out_specs=VMEM,
        compiler_params=pltpu.CompilerParams(vmem_limit_bytes=8 * MIB),
        name="row_phasor",
    )(rows, power)


def exchange(x, axes):
    return lax.all_to_all(x, axes, 0, 0, tiled=True)


def spread(x, axes, count):
    return exchange(jnp.broadcast_to(x[None], (count,) + x.shape), axes)


def total_of(x):
    return jnp.sum(x.astype(F32), 0)


def swap_cores(x):
    return lax.ppermute(x, "c", [(0, 1), (1, 0)])


def local(field_in, target, mask_old, scales):
    fld = field_in[0, 0]
    tgt = target[0, 0]
    core = lax.axis_index("c").reshape(1)
    mode = lax.axis_index(MODE).reshape(1)
    ar, ai, keep, send = call_back(scales, core, tgt, mask_old, fld)
    half = (keep + swap_cores(send).astype(F32)).astype(BF)
    part = total_of(exchange(half.reshape(16, 32, N), WAVE)).astype(BF)
    part = total_of(spread(part, ("y", "xh"), 16)).astype(BF)
    own = spread(part, WAVE, 16)
    other = swap_cores(own)
    mask_one, keep, send = call_ahead(core, mode, own, other, ar, ai, tgt, fld)
    half = (keep + swap_cores(send).astype(F32)).astype(BF)
    part = total_of(exchange(half, ("y", "xh"))).astype(BF)
    rows, power = call_power(spread(part, WAVE, 16))
    return mask_one, call_phasor(rows, exchange(power, MODE))


def solution(mesh):
    fine = Mesh(mesh.devices.reshape(SIZES), AXES)
    data = P(WAVE, MODE, None, None, None)
    rows = P(None, MODE, None)
    return jax.shard_map(
        local,
        mesh=fine,
        in_specs=(data, data, P(), P(WAVE)),
        out_specs=(rows, rows),
        check_vma=False,
    )
```

```python
import jax
import jax.numpy as jnp
from jax import lax
from jax.experimental import pallas as pl
from jax.experimental.pallas import tpu as pltpu
from jax.sharding import Mesh, PartitionSpec as P

N = 512
BF = jnp.bfloat16
F32 = jnp.float32
AXES = ("y", "xh", "c", "xl", "z")
SIZES = (8, 2, 2, 2, 8)
MODE = ("y", "xh", "c")
WAVE = ("xl", "z")
MIB = 1024 * 1024
BLK = 128


def dot(a, b):
    return jnp.dot(a, b, preferred_element_type=F32)


def chirp_into(scale, ar, ai):
    lane = lax.broadcasted_iota(jnp.int32, (8, 2 * N), 1)
    diff = (lane - N).astype(F32)
    angle = jnp.float32(jnp.pi) * scale * diff * diff / N
    factor = jnp.float32(N) ** (-0.5)
    for ref, fn in ((ar, jnp.cos), (ai, jnp.sin)):
        line = fn(angle) * factor
        for d in range(-3, 4):
            start = N + BLK * d - BLK
            window = line[0:1, start : start + 2 * BLK]
            window = jnp.broadcast_to(window, (BLK, 2 * BLK))
            rolled = pltpu.roll(window, BLK, 1, stride=1, stride_axis=0)
            block = rolled[:, :BLK].astype(BF)
            for row in range(4):
                col = row + d
                if 0 <= col < 4:
                    ref[row * BLK : (row + 1) * BLK, col * BLK : (col + 1) * BLK] = block


def back_kernel(scale_ref, core_ref, tgt_hbm, old_hbm, fld_hbm, ar, ai, keep, send, tgt, old, fld, z_s, sems):
    copies = [
        pltpu.make_async_copy(src, dst, sems.at[i])
        for i, (src, dst) in enumerate(((tgt_hbm, tgt), (old_hbm, old), (fld_hbm, fld)))
    ]
    for copy in copies:
        copy.start()
    chirp_into(scale_ref[0], ar, ai)
    copies[0].wait()
    copies[1].wait()
    for r in range(0, N, BLK):
        rows = slice(r, r + BLK)
        br = tgt[0, rows].astype(F32)
        bi = tgt[1, rows].astype(F32)
        mr = old[0, rows].astype(F32)
        mi = old[1, rows].astype(F32)
        cr = (br * mr + bi * mi).astype(BF)
        ci = (bi * mr - br * mi).astype(BF)
        z_s[0, rows] = (dot(cr, ar[...]) + dot(ci, ai[...])).astype(BF)
        z_s[1, rows] = (dot(ci, ar[...]) - dot(cr, ai[...])).astype(BF)
    copies[2].wait()
    first = core_ref[0] == 0
    for r in range(0, N, BLK):
        rows = slice(r, r + BLK)
        kr = ar[rows]
        ki = ai[rows]
        back_r = dot(kr, z_s[0]) + dot(ki, z_s[1])
        back_i = dot(kr, z_s[1]) - dot(ki, z_s[0])
        fr = fld[0, rows].astype(F32)
        fi = fld[1, rows].astype(F32)
        term_r = back_r * fr + back_i * fi
        term_i = back_i * fr - back_r * fi
        keep[rows] = jnp.where(first, term_r, term_i)
        send[rows] = jnp.where(first, term_i, term_r).astype(BF)


def ahead_kernel(core_ref, mode_ref, own, other, ar, ai, tgt, fld, mask_out, keep, send, mask, z_s):
    first = core_ref[0] == 0
    total = jnp.zeros((32, N), F32)
    for r in range(16):
        a = own[r].astype(F32)
        b = other[r].astype(F32)
        total = total + (a * a + b * b)
    bias = jnp.sum(total) / (N * N) + 1e-06
    for r in range(0, N, BLK):
        rows = slice(r, r + BLK)
        a = own[r // 32 : (r + BLK) // 32].reshape(BLK, N).astype(F32)
        b = other[r // 32 : (r + BLK) // 32].reshape(BLK, N).astype(F32)
        factor = lax.rsqrt(a * a + b * b + bias)
        a = a * factor
        b = b * factor
        mr = jnp.where(first, a, b).astype(BF)
        mi = jnp.where(first, b, a).astype(BF)
        mask[0, rows] = mr
        mask[1, rows] = mi
        mr = mr.astype(F32)
        mi = mi.astype(F32)
        fr = fld[0, rows].astype(F32)
        fi = fld[1, rows].astype(F32)
        gr = (fr * mr - fi * mi).astype(BF)
        gi = (fr * mi + fi * mr).astype(BF)
        z_s[0, rows] = (dot(gr, ar[...]) - dot(gi, ai[...])).astype(BF)
        z_s[1, rows] = (dot(gi, ar[...]) + dot(gr, ai[...])).astype(BF)
    start = pl.multiple_of(mode_ref[0] * 16, 16)
    mask_out[0] = mask[0, pl.ds(start, 16)]
    mask_out[1] = mask[1, pl.ds(start, 16)]
    for r in range(0, N, BLK):
        rows = slice(r, r + BLK)
        kr = ar[rows]
        ki = ai[rows]
        ahead_r = dot(kr, z_s[0]) - dot(ki, z_s[1])
        ahead_i = dot(kr, z_s[1]) + dot(ki, z_s[0])
        br = tgt[0, rows].astype(F32)
        bi = tgt[1, rows].astype(F32)
        term_r = br * ahead_r + bi * ahead_i
        term_i = bi * ahead_r - br * ahead_i
        for low in range(BLK // 32):
            q = r // 32 + low
            for w in range(16):
                part, half, col = w // 8, w // 4 % 2, w % 4
                term = (term_r, term_i)[part][:, col * 128 : (col + 1) * 128]
                even = term[low * 32 + half * 8 : low * 32 + half * 8 + 8]
                odd = term[low * 32 + 16 + half * 8 : low * 32 + 24 + half * 8]
                i = jnp.where(first, q, w)
                j = jnp.where(first, w, q)
                keep[i, j] = jnp.where(first, even, odd)
                send[j, i] = jnp.where(first, odd, even).astype(BF)


def power_kernel(mode_ref, parts, tiles, message):
    total = parts[0].astype(F32)
    for k in range(1, 16):
        total = total + parts[k].astype(F32)
    tiles[...] = total
    power = jnp.broadcast_to(jnp.sum(total * total), (8, 128))
    mine = tiles[mode_ref[0] // 2]
    for k in range(16):
        message[k, 0:8] = mine
        message[k, 8:16] = power


def phasor_kernel(core_ref, tiles, arrived, power, other, out, full):
    first = core_ref[0] == 0
    bias = (power[...] + other[...]) / (N * N) + 1e-06
    for half in range(2):
        for col in range(4):
            k = half * 4 + col
            a = jnp.where(first, tiles[k], arrived[k, 0:8])
            b = jnp.where(first, tiles[k + 8], arrived[k + 8, 0:8])
            factor = lax.rsqrt(a * a + b * b + bias)
            full[0, half * 8 : half * 8 + 8, col * 128 : (col + 1) * 128] = a * factor
            full[1, half * 8 : half * 8 + 8, col * 128 : (col + 1) * 128] = b * factor
    out[...] = full[...].astype(BF)


HBM = pl.BlockSpec(memory_space=pltpu.HBM)
SMEM = pl.BlockSpec(memory_space=pltpu.SMEM)
VMEM = pl.BlockSpec(memory_space=pltpu.VMEM)


def call_back(scale, core, tgt, old, fld):
    return pl.pallas_call(
        back_kernel,
        out_shape=(
            jax.ShapeDtypeStruct((N, N), BF),
            jax.ShapeDtypeStruct((N, N), BF),
            jax.ShapeDtypeStruct((N, N), F32),
            jax.ShapeDtypeStruct((N, N), BF),
        ),
        in_specs=[SMEM, SMEM, HBM, HBM, HBM],
        out_specs=(VMEM,) * 4,
        scratch_shapes=[
            pltpu.VMEM((2, N, N), BF),
            pltpu.VMEM((2, N, N), BF),
            pltpu.VMEM((2, N, N), BF),
            pltpu.VMEM((2, N, N), BF),
            pltpu.SemaphoreType.DMA((3,)),
        ],
        compiler_params=pltpu.CompilerParams(vmem_limit_bytes=16 * MIB),
        name="back_margin",
    )(scale, core, tgt, old, fld)


def call_ahead(core, mode, own, other, ar, ai, tgt, fld):
    return pl.pallas_call(
        ahead_kernel,
        out_shape=(
            jax.ShapeDtypeStruct((2, 16, N), BF),
            jax.ShapeDtypeStruct((16, 16, 8, 128), F32),
            jax.ShapeDtypeStruct((16, 16, 8, 128), BF),
        ),
        in_specs=[SMEM, SMEM] + [VMEM] * 6,
        out_specs=(VMEM,) * 3,
        scratch_shapes=[pltpu.VMEM((2, N, N), BF), pltpu.VMEM((2, N, N), BF)],
        compiler_params=pltpu.CompilerParams(vmem_limit_bytes=16 * MIB),
        name="ahead_margin",
    )(core, mode, own, other, ar, ai, tgt, fld)


def call_power(mode, parts):
    return pl.pallas_call(
        power_kernel,
        out_shape=(jax.ShapeDtypeStruct((16, 8, 128), F32), jax.ShapeDtypeStruct((16, 16, 128), F32)),
        in_specs=[SMEM, VMEM],
        out_specs=(VMEM, VMEM),
        compiler_params=pltpu.CompilerParams(vmem_limit_bytes=8 * MIB),
        name="tile_power",
    )(mode, parts)


def call_phasor(core, tiles, arrived, power, other):
    return pl.pallas_call(
        phasor_kernel,
        out_shape=jax.ShapeDtypeStruct((2, 16, N), BF),
        in_specs=[SMEM] + [VMEM] * 4,
        out_specs=VMEM,
        scratch_shapes=[pltpu.VMEM((2, 16, N), F32)],
        compiler_params=pltpu.CompilerParams(vmem_limit_bytes=8 * MIB),
        name="tile_phasor",
    )(core, tiles, arrived, power, other)


def device(y, xh, c, xl, z):
    return (((y * 2 + xh) * 2 + c) * 2 + xl) * 8 + z


def ring_groups(core):
    rows = [(y, xh) for y in range(8) for xh in range(2)]
    waves = [(xl, z) for xl in range(2) for z in range(8)]
    groups = [[device(*q, core, *w) for q in rows] for w in waves]
    return groups + [[device(*q, 1 - core, *w) for w in waves] for q in rows]


RING_A = ring_groups(0)
RING_B = ring_groups(1)


def exchange(x, groups):
    return lax.all_to_all(x, AXES, 0, 0, tiled=True, axis_index_groups=groups)


def spread(x, groups):
    return exchange(jnp.broadcast_to(x[None], (16,) + x.shape), groups)


def total_of(x):
    return jnp.sum(x.astype(F32), 0).astype(BF)


def swap_cores(x):
    return lax.ppermute(x, "c", [(0, 1), (1, 0)])


def local(field_in, target, mask_old, scales):
    fld = field_in[0, 0]
    tgt = target[0, 0]
    core = lax.axis_index("c").reshape(1)
    mode = lax.axis_index(MODE).reshape(1)
    ar, ai, keep, send = call_back(scales, core, tgt, mask_old, fld)
    half = (keep + swap_cores(send).astype(F32)).astype(BF)
    part = total_of(exchange(half.reshape(16, 32, N), RING_A))
    part = total_of(spread(part, RING_B))
    own = spread(part, RING_A)
    other = swap_cores(own)
    mask_one, keep, send = call_ahead(core, mode, own, other, ar, ai, tgt, fld)
    half = (keep + swap_cores(send).astype(F32)).astype(BF)
    part = total_of(exchange(half, RING_A))
    tiles, message = call_power(mode, spread(part, RING_B))
    arrived = exchange(message, RING_A)
    power = jnp.sum(arrived[:, 8:], 0)
    return mask_one, call_phasor(core, tiles, arrived, power, swap_cores(power))


def solution(mesh):
    fine = Mesh(mesh.devices.reshape(SIZES), AXES)
    data = P(WAVE, MODE, None, None, None)
    rows = P(None, MODE, None)
    return jax.shard_map(
        local,
        mesh=fine,
        in_specs=(data, data, P(), P(WAVE)),
        out_specs=(rows, rows),
        check_vma=False,
    )
```

```python
import jax
import jax.numpy as jnp
from jax import lax
from jax.experimental import pallas as pl
from jax.experimental.pallas import tpu as pltpu
from jax.sharding import Mesh, PartitionSpec as P

N = 512
BF = jnp.bfloat16
F32 = jnp.float32
AXES = ("y", "xh", "c", "xl", "z")
SIZES = (8, 2, 2, 2, 8)
MODE = ("y", "xh", "c")
WAVE = ("xl", "z")
MIB = 1024 * 1024
BLK = 128
CHUNK = 16


def dot(a, b):
    return jnp.dot(a, b, preferred_element_type=F32)


def chirp_into(scale, ar, ai):
    lane = lax.broadcasted_iota(jnp.int32, (8, 2 * N), 1)
    diff = (lane - N).astype(F32)
    angle = jnp.float32(jnp.pi) * scale * diff * diff / N
    factor = jnp.float32(N) ** (-0.5)
    for ref, fn in ((ar, jnp.cos), (ai, jnp.sin)):
        line = fn(angle) * factor
        for d in range(-3, 4):
            start = N + BLK * d - BLK
            window = line[0:1, start : start + 2 * BLK]
            window = jnp.broadcast_to(window, (BLK, 2 * BLK))
            rolled = pltpu.roll(window, BLK, 1, stride=1, stride_axis=0)
            block = rolled[:, :BLK].astype(BF)
            for row in range(4):
                col = row + d
                if 0 <= col < 4:
                    ref[row * BLK : (row + 1) * BLK, col * BLK : (col + 1) * BLK] = block


def chirp_kernel(scale_ref, after, a):
    chirp_into(scale_ref[0], a.at[0], a.at[1])


def back_kernel(scale_ref, core_ref, tgt_hbm, old_hbm, fld_hbm, keep_hbm, send_hbm,
                tgt, old, fld, a, z_s, keep, send, in_sems, out_sems):
    arrive = [
        pltpu.make_async_copy(src.at[part], dst.at[part], in_sems.at[2 * i + part])
        for i, (src, dst) in enumerate(((tgt_hbm, tgt), (old_hbm, old), (fld_hbm, fld)))
        for part in range(2)
    ]
    for copy in arrive:
        copy.start()
    chirp_into(scale_ref[0], a.at[0], a.at[1])
    leave = []
    for copy in arrive[:4]:
        copy.wait()
    for r in range(0, N, BLK):
        rows = slice(r, r + BLK)
        br = tgt[0, rows].astype(F32)
        bi = tgt[1, rows].astype(F32)
        mr = old[0, rows].astype(F32)
        mi = old[1, rows].astype(F32)
        cr = (br * mr + bi * mi).astype(BF)
        ci = (bi * mr - br * mi).astype(BF)
        z_s[0, rows] = (dot(cr, a[0]) + dot(ci, a[1])).astype(BF)
        z_s[1, rows] = (dot(ci, a[0]) - dot(cr, a[1])).astype(BF)
    for copy in arrive[4:]:
        copy.wait()
    first = core_ref[0] == 0
    for r in range(0, N, BLK):
        rows = slice(r, r + BLK)
        kr = a[0, rows]
        ki = a[1, rows]
        back_r = dot(kr, z_s[0]) + dot(ki, z_s[1])
        back_i = dot(kr, z_s[1]) - dot(ki, z_s[0])
        fr = fld[0, rows].astype(F32)
        fi = fld[1, rows].astype(F32)
        term_r = back_r * fr + back_i * fi
        term_i = back_i * fr - back_r * fi
        send[rows] = jnp.where(first, term_i, term_r).astype(BF)
        keep[rows] = jnp.where(first, term_r, term_i).astype(BF)
        for src, dst in ((send, send_hbm), (keep, keep_hbm)):
            copy = pltpu.make_async_copy(src.at[rows], dst.at[rows], out_sems.at[len(leave)])
            copy.start()
            leave.append(copy)
    for copy in leave:
        copy.wait()


def ahead_kernel(core_ref, mode_ref, own, other, a_ref, tgt, fld, mask_out, keep, send, mask, z_s):
    first = core_ref[0] == 0
    total = jnp.zeros((CHUNK, N), F32)
    for r in range(N // CHUNK):
        a = own[r].astype(F32)
        b = other[r].astype(F32)
        total = total + (a * a + b * b)
    bias = jnp.sum(total) / (N * N) + 1e-06
    for r in range(0, N, BLK):
        rows = slice(r, r + BLK)
        a = own[r // CHUNK : (r + BLK) // CHUNK].reshape(BLK, N).astype(F32)
        b = other[r // CHUNK : (r + BLK) // CHUNK].reshape(BLK, N).astype(F32)
        factor = lax.rsqrt(a * a + b * b + bias)
        a = a * factor
        b = b * factor
        mr = jnp.where(first, a, b).astype(BF)
        mi = jnp.where(first, b, a).astype(BF)
        mask[0, rows] = mr
        mask[1, rows] = mi
        mr = mr.astype(F32)
        mi = mi.astype(F32)
        fr = fld[0, rows].astype(F32)
        fi = fld[1, rows].astype(F32)
        gr = (fr * mr - fi * mi).astype(BF)
        gi = (fr * mi + fi * mr).astype(BF)
        z_s[0, rows] = (dot(gr, a_ref[0]) - dot(gi, a_ref[1])).astype(BF)
        z_s[1, rows] = (dot(gi, a_ref[0]) + dot(gr, a_ref[1])).astype(BF)
    start = pl.multiple_of(mode_ref[0] * 16, 16)
    mask_out[0] = mask[0, pl.ds(start, 16)]
    mask_out[1] = mask[1, pl.ds(start, 16)]
    for r in range(0, N, BLK):
        rows = slice(r, r + BLK)
        kr = a_ref[0, rows]
        ki = a_ref[1, rows]
        ahead_r = dot(kr, z_s[0]) - dot(ki, z_s[1])
        ahead_i = dot(kr, z_s[1]) + dot(ki, z_s[0])
        br = tgt[0, rows].astype(F32)
        bi = tgt[1, rows].astype(F32)
        term_r = br * ahead_r + bi * ahead_i
        term_i = bi * ahead_r - br * ahead_i
        for low in range(BLK // 32):
            q = r // 32 + low
            for w in range(16):
                part, half, col = w // 8, w // 4 % 2, w % 4
                term = (term_r, term_i)[part][:, col * 128 : (col + 1) * 128]
                even = term[low * 32 + half * 8 : low * 32 + half * 8 + 8]
                odd = term[low * 32 + 16 + half * 8 : low * 32 + 24 + half * 8]
                i = jnp.where(first, q, w)
                j = jnp.where(first, w, q)
                keep[i, j] = jnp.where(first, even, odd)
                send[j, i] = jnp.where(first, odd, even).astype(BF)


def power_kernel(mode_ref, parts, tiles, message):
    total = parts[0].astype(F32)
    for k in range(1, 16):
        total = total + parts[k].astype(F32)
    tiles[...] = total
    power = jnp.broadcast_to(jnp.sum(total * total), (8, 128))
    high = power.astype(BF).astype(F32)
    row = lax.broadcasted_iota(jnp.int32, (8, 128), 0)
    power = jnp.where(row < 4, high, power - high)
    mine = jnp.concatenate([tiles[mode_ref[0] // 2], power], 0).astype(BF)
    for k in range(16):
        message[k] = mine


def phasor_kernel(core_ref, tiles, arrived, power, other, out, full):
    first = core_ref[0] == 0
    bias = jnp.sum(power[...] + other[...], 0, keepdims=True) / (4 * N * N) + 1e-06
    for half in range(2):
        for col in range(4):
            k = half * 4 + col
            a = jnp.where(first, tiles[k], arrived[k].astype(F32)[0:8])
            b = jnp.where(first, tiles[k + 8], arrived[k + 8].astype(F32)[0:8])
            factor = lax.rsqrt(a * a + b * b + bias)
            full[0, half * 8 : half * 8 + 8, col * 128 : (col + 1) * 128] = a * factor
            full[1, half * 8 : half * 8 + 8, col * 128 : (col + 1) * 128] = b * factor
    out[...] = full[...].astype(BF)


HBM = pl.BlockSpec(memory_space=pltpu.HBM)
ANY = pl.BlockSpec(memory_space=pl.ANY)
SMEM = pl.BlockSpec(memory_space=pltpu.SMEM)
VMEM = pl.BlockSpec(memory_space=pltpu.VMEM)


def call_chirp(scale, after):
    return pl.pallas_call(
        chirp_kernel,
        out_shape=jax.ShapeDtypeStruct((2, N, N), BF),
        in_specs=[SMEM, ANY],
        out_specs=VMEM,
        compiler_params=pltpu.CompilerParams(vmem_limit_bytes=8 * MIB),
        cost_estimate=pl.CostEstimate(flops=10**9, bytes_accessed=2**20, transcendentals=2**12),
        name="chirp",
    )(scale, after)


def call_back(scale, core, tgt, old, fld):
    blocks = N // BLK
    return pl.pallas_call(
        back_kernel,
        out_shape=(
            jax.ShapeDtypeStruct((N, N), BF),
            jax.ShapeDtypeStruct((N, N), BF),
        ),
        in_specs=[SMEM, SMEM, HBM, HBM, HBM],
        out_specs=(HBM,) * 2,
        scratch_shapes=[pltpu.VMEM((2, N, N), BF)] * 5
        + [
            pltpu.VMEM((N, N), BF),
            pltpu.VMEM((N, N), BF),
            pltpu.SemaphoreType.DMA((6,)),
            pltpu.SemaphoreType.DMA((2 * blocks,)),
        ],
        compiler_params=pltpu.CompilerParams(vmem_limit_bytes=58 * MIB),
        name="back_margin",
    )(scale, core, tgt, old, fld)


def call_ahead(core, mode, own, other, a, tgt, fld):
    return pl.pallas_call(
        ahead_kernel,
        out_shape=(
            jax.ShapeDtypeStruct((2, 16, N), BF),
            jax.ShapeDtypeStruct((16, 16, 8, 128), F32),
            jax.ShapeDtypeStruct((16, 16, 8, 128), BF),
        ),
        in_specs=[SMEM, SMEM] + [VMEM] * 5,
        out_specs=(VMEM,) * 3,
        scratch_shapes=[pltpu.VMEM((2, N, N), BF), pltpu.VMEM((2, N, N), BF)],
        compiler_params=pltpu.CompilerParams(vmem_limit_bytes=16 * MIB),
        name="ahead_margin",
    )(core, mode, own, other, a, tgt, fld)


def call_power(mode, parts):
    return pl.pallas_call(
        power_kernel,
        out_shape=(jax.ShapeDtypeStruct((16, 8, 128), F32), jax.ShapeDtypeStruct((16, 16, 128), BF)),
        in_specs=[SMEM, VMEM],
        out_specs=(VMEM, VMEM),
        compiler_params=pltpu.CompilerParams(vmem_limit_bytes=8 * MIB),
        name="tile_power",
    )(mode, parts)


def call_phasor(core, tiles, arrived, power, other):
    return pl.pallas_call(
        phasor_kernel,
        out_shape=jax.ShapeDtypeStruct((2, 16, N), BF),
        in_specs=[SMEM] + [VMEM] * 4,
        out_specs=VMEM,
        scratch_shapes=[pltpu.VMEM((2, 16, N), F32)],
        compiler_params=pltpu.CompilerParams(vmem_limit_bytes=8 * MIB),
        name="tile_phasor",
    )(core, tiles, arrived, power, other)


def device(y, xh, c, xl, z):
    return (((y * 2 + xh) * 2 + c) * 2 + xl) * 8 + z


def ring_groups(core, rows, waves):
    def groups(own, cross, c, make):
        return [[device(**make(i, j), c=c) for i in own] for j in cross]

    flat = lambda i, j: {**i, **j}
    return groups(rows, waves, core, flat) + groups(waves, rows, 1 - core, flat)


def points(**sizes):
    found = [{}]
    for name, size in sizes.items():
        found = [{**point, name: k} for point in found for k in range(size)]
    return found


def wide_groups():
    x = points(xh=2, xl=2)
    y, z = points(y=8), points(z=8)
    first = [[device(**i, **k, **j, c=0) for i in y for k in x] for j in z]
    return first + [[device(**i, **k, **j, c=1) for j in z for k in x] for i in y]


def narrow_groups():
    x = points(xh=2, xl=2)
    y, z = points(y=8), points(z=8)
    first = [[device(**i, **k, **j, c=0) for j in z] for i in y for k in x]
    return first + [[device(**i, **k, **j, c=1) for i in y] for j in z for k in x]


ROWS, WAVES = points(y=8, xh=2), points(xl=2, z=8)
RING_A = ring_groups(0, ROWS, WAVES)
RING_B = ring_groups(1, ROWS, WAVES)
WIDE = wide_groups()
NARROW = narrow_groups()


def exchange(x, groups):
    return lax.all_to_all(x, AXES, 0, 0, tiled=True, axis_index_groups=groups)


def spread(x, groups):
    return exchange(jnp.broadcast_to(x[None], (len(groups[0]),) + x.shape), groups)


def total_of(x):
    return jnp.sum(x.astype(F32), 0).astype(BF)


def swap_cores(x):
    return lax.ppermute(x, "c", [(0, 1), (1, 0)])


def local(field_in, target, mask_old, scales):
    fld = field_in[0, 0]
    tgt = target[0, 0]
    core = lax.axis_index("c").reshape(1)
    mode = lax.axis_index(MODE).reshape(1)
    keep, send = call_back(scales, core, tgt, mask_old, fld)
    half = (keep.astype(F32) + swap_cores(send).astype(F32)).astype(BF)
    part = total_of(exchange(half.reshape(N // CHUNK, CHUNK, N), WIDE))
    part = total_of(spread(part, NARROW))
    own = spread(part, WIDE)
    other = swap_cores(own)
    a = call_chirp(scales, own)
    mask_one, keep, send = call_ahead(core, mode, own, other, a, tgt, fld)
    half = (keep + swap_cores(send).astype(F32)).astype(BF)
    part = total_of(exchange(half, RING_A))
    tiles, message = call_power(mode, spread(part, RING_B))
    arrived = exchange(message, RING_A)
    power = jnp.sum(arrived[:, 8:].astype(F32), 0)
    return mask_one, call_phasor(core, tiles, arrived, power, swap_cores(power))


def solution(mesh):
    fine = Mesh(mesh.devices.reshape(SIZES), AXES)
    data = P(WAVE, MODE, None, None, None)
    rows = P(None, MODE, None)
    return jax.shard_map(
        local,
        mesh=fine,
        in_specs=(data, data, P(), P(WAVE)),
        out_specs=(rows, rows),
        check_vma=False,
    )
```

```python
import jax
import jax.numpy as jnp
from jax import lax
from jax.experimental import pallas as pl
from jax.experimental.pallas import tpu as pltpu
from jax.sharding import Mesh, PartitionSpec as P

N = 512
BF = jnp.bfloat16
F32 = jnp.float32
AXES = ("y", "xh", "c", "xl", "z")
SIZES = (8, 2, 2, 2, 8)
MODE = ("y", "xh", "c")
WAVE = ("xl", "z")
MIB = 1024 * 1024
BLK = 128
CHUNK = 16


def dot(a, b):
    return jnp.dot(a, b, preferred_element_type=F32)


def chirp_into(scale, ar, ai):
    lane = lax.broadcasted_iota(jnp.int32, (8, 2 * N), 1)
    diff = (lane - N).astype(F32)
    angle = jnp.float32(jnp.pi) * scale * diff * diff / N
    factor = jnp.float32(N) ** (-0.5)
    for ref, fn in ((ar, jnp.cos), (ai, jnp.sin)):
        line = fn(angle) * factor
        for d in range(-3, 4):
            start = N + BLK * d - BLK
            window = line[0:1, start : start + 2 * BLK]
            window = jnp.broadcast_to(window, (BLK, 2 * BLK))
            rolled = pltpu.roll(window, BLK, 1, stride=1, stride_axis=0)
            block = rolled[:, :BLK].astype(BF)
            for row in range(4):
                col = row + d
                if 0 <= col < 4:
                    ref[row * BLK : (row + 1) * BLK, col * BLK : (col + 1) * BLK] = block


def chirp_kernel(scale_ref, after, a):
    chirp_into(scale_ref[0], a.at[0], a.at[1])


def back_kernel(scale_ref, core_ref, tgt_hbm, old_hbm, fld_hbm, keep, send, tgt, old, fld, a, z_s, sems):
    blocks = [slice(r, r + BLK) for r in range(0, N, BLK)]
    arrive = []
    for pairs in (((tgt_hbm, tgt), (old_hbm, old)), ((fld_hbm, fld),)):
        for rows in blocks:
            for src, dst in pairs:
                arrive.append(pltpu.make_async_copy(src.at[:, rows], dst.at[:, rows], sems.at[len(arrive)]))
    for copy in arrive:
        copy.start()
    chirp_into(scale_ref[0], a.at[0], a.at[1])
    for i, rows in enumerate(blocks):
        arrive[2 * i].wait()
        arrive[2 * i + 1].wait()
        br = tgt[0, rows].astype(F32)
        bi = tgt[1, rows].astype(F32)
        mr = old[0, rows].astype(F32)
        mi = old[1, rows].astype(F32)
        cr = (br * mr + bi * mi).astype(BF)
        ci = (bi * mr - br * mi).astype(BF)
        z_s[0, rows] = (dot(cr, a[0]) + dot(ci, a[1])).astype(BF)
        z_s[1, rows] = (dot(ci, a[0]) - dot(cr, a[1])).astype(BF)
    first = core_ref[0] == 0
    for i, rows in enumerate(blocks):
        kr = a[0, rows]
        ki = a[1, rows]
        back_r = dot(kr, z_s[0]) + dot(ki, z_s[1])
        back_i = dot(kr, z_s[1]) - dot(ki, z_s[0])
        arrive[2 * len(blocks) + i].wait()
        fr = fld[0, rows].astype(F32)
        fi = fld[1, rows].astype(F32)
        term_r = back_r * fr + back_i * fi
        term_i = back_i * fr - back_r * fi
        send[rows] = jnp.where(first, term_i, term_r).astype(BF)
        keep[rows] = jnp.where(first, term_r, term_i).astype(BF)


def ahead_rows(owner, by_mode, a_ref, z_s, tgt, out):
    def gather(ref, part, first_q):
        starts = [pl.multiple_of(32 * (first_q + k) + 16 * owner, 16) for k in range(8)]
        return jnp.concatenate([ref[part, pl.ds(start, 16)] for start in starts], 0)

    for first_q in (0, 8):
        kr = gather(a_ref, 0, first_q)
        ki = gather(a_ref, 1, first_q)
        ahead_r = dot(kr, z_s[0]) - dot(ki, z_s[1])
        ahead_i = dot(kr, z_s[1]) + dot(ki, z_s[0])
        br = gather(tgt, 0, first_q).astype(F32)
        bi = gather(tgt, 1, first_q).astype(F32)
        terms = (br * ahead_r + bi * ahead_i, bi * ahead_r - br * ahead_i)
        for low in range(8):
            q = first_q + low
            for w in range(16):
                part, half, col = w // 8, w // 4 % 2, w % 4
                top = low * 16 + half * 8
                tile = terms[part][top : top + 8, col * 128 : (col + 1) * 128]
                out[jnp.where(by_mode, q, w), jnp.where(by_mode, w, q)] = tile.astype(out.dtype)


def ahead_kernel(core_ref, mode_ref, own, other, a_ref, tgt, fld, mask_out, z_s, send, mask):
    first = core_ref[0] == 0
    total = jnp.zeros((CHUNK, N), F32)
    for r in range(N // CHUNK):
        a = own[r].astype(F32)
        b = other[r].astype(F32)
        total = total + (a * a + b * b)
    bias = jnp.sum(total) / (N * N) + 1e-06
    for r in range(0, N, BLK):
        rows = slice(r, r + BLK)
        a = own[r // CHUNK : (r + BLK) // CHUNK].reshape(BLK, N).astype(F32)
        b = other[r // CHUNK : (r + BLK) // CHUNK].reshape(BLK, N).astype(F32)
        factor = lax.rsqrt(a * a + b * b + bias)
        a = a * factor
        b = b * factor
        mr = jnp.where(first, a, b).astype(BF)
        mi = jnp.where(first, b, a).astype(BF)
        mask[0, rows] = mr
        mask[1, rows] = mi
        mr = mr.astype(F32)
        mi = mi.astype(F32)
        fr = fld[0, rows].astype(F32)
        fi = fld[1, rows].astype(F32)
        gr = (fr * mr - fi * mi).astype(BF)
        gi = (fr * mi + fi * mr).astype(BF)
        z_s[0, rows] = (dot(gr, a_ref[0]) - dot(gi, a_ref[1])).astype(BF)
        z_s[1, rows] = (dot(gi, a_ref[0]) + dot(gr, a_ref[1])).astype(BF)
    start = pl.multiple_of(mode_ref[0] * 16, 16)
    mask_out[0] = mask[0, pl.ds(start, 16)]
    mask_out[1] = mask[1, pl.ds(start, 16)]
    ahead_rows(1 - core_ref[0], core_ref[0] != 0, a_ref, z_s, tgt, send)


def keep_kernel(core_ref, a_ref, z_s, tgt, keep):
    ahead_rows(core_ref[0], core_ref[0] == 0, a_ref, z_s, tgt, keep)


def power_kernel(mode_ref, parts, tiles, message):
    total = parts[0].astype(F32)
    for k in range(1, 16):
        total = total + parts[k].astype(F32)
    tiles[...] = total
    power = jnp.broadcast_to(jnp.sum(total * total), (8, 128))
    high = power.astype(BF).astype(F32)
    row = lax.broadcasted_iota(jnp.int32, (8, 128), 0)
    power = jnp.where(row < 4, high, power - high)
    mine = jnp.concatenate([tiles[mode_ref[0] // 2], power], 0).astype(BF)
    for k in range(16):
        message[k] = mine


def phasor_kernel(core_ref, tiles, arrived, power, other, out, full):
    first = core_ref[0] == 0
    bias = jnp.sum(power[...] + other[...], 0, keepdims=True) / (4 * N * N) + 1e-06
    for half in range(2):
        for col in range(4):
            k = half * 4 + col
            a = jnp.where(first, tiles[k], arrived[k].astype(F32)[0:8])
            b = jnp.where(first, tiles[k + 8], arrived[k + 8].astype(F32)[0:8])
            factor = lax.rsqrt(a * a + b * b + bias)
            full[0, half * 8 : half * 8 + 8, col * 128 : (col + 1) * 128] = a * factor
            full[1, half * 8 : half * 8 + 8, col * 128 : (col + 1) * 128] = b * factor
    out[...] = full[...].astype(BF)


HBM = pl.BlockSpec(memory_space=pltpu.HBM)
ANY = pl.BlockSpec(memory_space=pl.ANY)
SMEM = pl.BlockSpec(memory_space=pltpu.SMEM)
VMEM = pl.BlockSpec(memory_space=pltpu.VMEM)


def call_chirp(scale, after):
    return pl.pallas_call(
        chirp_kernel,
        out_shape=jax.ShapeDtypeStruct((2, N, N), BF),
        in_specs=[SMEM, ANY],
        out_specs=VMEM,
        compiler_params=pltpu.CompilerParams(vmem_limit_bytes=8 * MIB),
        cost_estimate=pl.CostEstimate(flops=10**9, bytes_accessed=2**20, transcendentals=2**12),
        name="chirp",
    )(scale, after)


def call_back(scale, core, tgt, old, fld):
    blocks = N // BLK
    return pl.pallas_call(
        back_kernel,
        out_shape=(
            jax.ShapeDtypeStruct((N, N), BF),
            jax.ShapeDtypeStruct((N, N), BF),
        ),
        in_specs=[SMEM, SMEM, HBM, HBM, HBM],
        out_specs=(VMEM,) * 2,
        scratch_shapes=[pltpu.VMEM((2, N, N), BF)] * 5
        + [
            pltpu.SemaphoreType.DMA((3 * blocks,)),
        ],
        compiler_params=pltpu.CompilerParams(vmem_limit_bytes=52 * MIB),
        name="back_margin",
    )(scale, core, tgt, old, fld)


def call_ahead(core, mode, own, other, a, tgt, fld):
    return pl.pallas_call(
        ahead_kernel,
        out_shape=(
            jax.ShapeDtypeStruct((2, 16, N), BF),
            jax.ShapeDtypeStruct((2, N, N), BF),
            jax.ShapeDtypeStruct((16, 16, 8, 128), BF),
        ),
        in_specs=[SMEM, SMEM] + [VMEM] * 5,
        out_specs=(VMEM,) * 3,
        scratch_shapes=[pltpu.VMEM((2, N, N), BF)],
        compiler_params=pltpu.CompilerParams(vmem_limit_bytes=16 * MIB),
        name="ahead_margin",
    )(core, mode, own, other, a, tgt, fld)


def call_keep(core, a, z, tgt):
    return pl.pallas_call(
        keep_kernel,
        out_shape=jax.ShapeDtypeStruct((16, 16, 8, 128), F32),
        in_specs=[SMEM] + [VMEM] * 3,
        out_specs=VMEM,
        compiler_params=pltpu.CompilerParams(vmem_limit_bytes=16 * MIB),
        cost_estimate=pl.CostEstimate(flops=2**30, bytes_accessed=2**22, transcendentals=0),
        name="keep_margin",
    )(core, a, z, tgt)


def call_power(mode, parts):
    return pl.pallas_call(
        power_kernel,
        out_shape=(jax.ShapeDtypeStruct((16, 8, 128), F32), jax.ShapeDtypeStruct((16, 16, 128), BF)),
        in_specs=[SMEM, VMEM],
        out_specs=(VMEM, VMEM),
        compiler_params=pltpu.CompilerParams(vmem_limit_bytes=8 * MIB),
        name="tile_power",
    )(mode, parts)


def call_phasor(core, tiles, arrived, power, other):
    return pl.pallas_call(
        phasor_kernel,
        out_shape=jax.ShapeDtypeStruct((2, 16, N), BF),
        in_specs=[SMEM] + [VMEM] * 4,
        out_specs=VMEM,
        scratch_shapes=[pltpu.VMEM((2, 16, N), F32)],
        compiler_params=pltpu.CompilerParams(vmem_limit_bytes=8 * MIB),
        name="tile_phasor",
    )(core, tiles, arrived, power, other)


def device(y, xh, c, xl, z):
    return (((y * 2 + xh) * 2 + c) * 2 + xl) * 8 + z


def ring_groups(core, rows, waves):
    def groups(own, cross, c, make):
        return [[device(**make(i, j), c=c) for i in own] for j in cross]

    flat = lambda i, j: {**i, **j}
    return groups(rows, waves, core, flat) + groups(waves, rows, 1 - core, flat)


def points(**sizes):
    found = [{}]
    for name, size in sizes.items():
        found = [{**point, name: k} for point in found for k in range(size)]
    return found


def wide_groups():
    x = points(xh=2, xl=2)
    y, z = points(y=8), points(z=8)
    first = [[device(**i, **k, **j, c=0) for i in y for k in x] for j in z]
    return first + [[device(**i, **k, **j, c=1) for j in z for k in x] for i in y]


def narrow_groups():
    x = points(xh=2, xl=2)
    y, z = points(y=8), points(z=8)
    first = [[device(**i, **k, **j, c=0) for j in z] for i in y for k in x]
    return first + [[device(**i, **k, **j, c=1) for i in y] for j in z for k in x]


ROWS, WAVES = points(y=8, xh=2), points(xl=2, z=8)
RING_A = ring_groups(0, ROWS, WAVES)
RING_B = ring_groups(1, ROWS, WAVES)
WIDE = wide_groups()
NARROW = narrow_groups()


def exchange(x, groups):
    return lax.all_to_all(x, AXES, 0, 0, tiled=True, axis_index_groups=groups)


def spread(x, groups):
    return exchange(jnp.broadcast_to(x[None], (len(groups[0]),) + x.shape), groups)


def total_of(x):
    return jnp.sum(x.astype(F32), 0).astype(BF)


def swap_cores(x):
    return lax.ppermute(x, "c", [(0, 1), (1, 0)])


def local(field_in, target, mask_old, scales):
    fld = field_in[0, 0]
    tgt = target[0, 0]
    core = lax.axis_index("c").reshape(1)
    mode = lax.axis_index(MODE).reshape(1)
    keep, send = call_back(scales, core, tgt, mask_old, fld)
    half = (keep.astype(F32) + swap_cores(send).astype(F32)).astype(BF)
    part = total_of(exchange(half.reshape(N // CHUNK, CHUNK, N), WIDE))
    part = total_of(spread(part, NARROW))
    own = spread(part, WIDE)
    other = swap_cores(own)
    a = call_chirp(scales, own)
    mask_one, middle, send = call_ahead(core, mode, own, other, a, tgt, fld)
    came = swap_cores(send)
    keep = call_keep(core, a, middle, tgt)
    half = (keep + came.astype(F32)).astype(BF)
    part = total_of(exchange(half, RING_A))
    tiles, message = call_power(mode, spread(part, RING_B))
    arrived = exchange(message, RING_A)
    power = jnp.sum(arrived[:, 8:].astype(F32), 0)
    return mask_one, call_phasor(core, tiles, arrived, power, swap_cores(power))


def solution(mesh):
    fine = Mesh(mesh.devices.reshape(SIZES), AXES)
    data = P(WAVE, MODE, None, None, None)
    rows = P(None, MODE, None)
    return jax.shard_map(
        local,
        mesh=fine,
        in_specs=(data, data, P(), P(WAVE)),
        out_specs=(rows, rows),
        check_vma=False,
    )
```

```python
import jax
import jax.numpy as jnp
from jax import lax
from jax.experimental import pallas as pl
from jax.experimental.pallas import tpu as pltpu
from jax.sharding import Mesh, PartitionSpec as P

N = 512
BF = jnp.bfloat16
F32 = jnp.float32
AXES = ("y", "xh", "c", "xl", "z")
SIZES = (8, 2, 2, 2, 8)
MODE = ("y", "xh", "c")
WAVE = ("xl", "z")
MIB = 1024 * 1024
BLK = 128
STEP = 256
CHUNK = 16


def dot(a, b):
    return jnp.dot(a, b, preferred_element_type=F32)


def both(left, right):
    rows = left.shape[1]
    stacked = left.reshape(2 * rows, N)
    p = dot(stacked, right[0])
    q = dot(stacked, right[1])
    return p[:rows], p[rows:], q[:rows], q[rows:]


def chirp_into(scale, ar, ai):
    lane = lax.broadcasted_iota(jnp.int32, (8, 2 * N), 1)
    diff = (lane - N).astype(F32)
    angle = jnp.float32(jnp.pi) * scale * diff * diff / N
    factor = jnp.float32(N) ** (-0.5)
    for ref, fn in ((ar, jnp.cos), (ai, jnp.sin)):
        line = fn(angle) * factor
        for d in range(-3, 4):
            start = N + BLK * d - BLK
            window = line[0:1, start : start + 2 * BLK]
            window = jnp.broadcast_to(window, (BLK, 2 * BLK))
            rolled = pltpu.roll(window, BLK, 1, stride=1, stride_axis=0)
            block = rolled[:, :BLK].astype(BF)
            for row in range(4):
                col = row + d
                if 0 <= col < 4:
                    ref[row * BLK : (row + 1) * BLK, col * BLK : (col + 1) * BLK] = block


def chirp_kernel(scale_ref, after, a):
    chirp_into(scale_ref[0], a.at[0], a.at[1])


def back_kernel(scale_ref, core_ref, tgt_hbm, old_hbm, fld_hbm, keep, send, tgt, old, fld, a, z_s, c_s, sems):
    blocks = [slice(r, r + STEP) for r in range(0, N, STEP)]
    arrive = []
    for pairs in (((tgt_hbm, tgt), (old_hbm, old)), ((fld_hbm, fld),)):
        for rows in blocks:
            for src, dst in pairs:
                arrive.append(pltpu.make_async_copy(src.at[:, rows], dst.at[:, rows], sems.at[len(arrive)]))
    for copy in arrive:
        copy.start()
    chirp_into(scale_ref[0], a.at[0], a.at[1])
    for i, rows in enumerate(blocks):
        arrive[2 * i].wait()
        arrive[2 * i + 1].wait()
        br = tgt[0, rows].astype(F32)
        bi = tgt[1, rows].astype(F32)
        mr = old[0, rows].astype(F32)
        mi = old[1, rows].astype(F32)
        c_s[0, rows] = (br * mr + bi * mi).astype(BF)
        c_s[1, rows] = (bi * mr - br * mi).astype(BF)
        rr, ir, ri, ii = both(c_s[:, rows], a)
        z_s[0, rows] = (rr + ii).astype(BF)
        z_s[1, rows] = (ir - ri).astype(BF)
    first = core_ref[0] == 0
    for i, rows in enumerate(blocks):
        rr, ir, ri, ii = both(a[:, rows], z_s)
        back_r = rr + ii
        back_i = ri - ir
        arrive[2 * len(blocks) + i].wait()
        fr = fld[0, rows].astype(F32)
        fi = fld[1, rows].astype(F32)
        term_r = back_r * fr + back_i * fi
        term_i = back_i * fr - back_r * fi
        send[rows] = jnp.where(first, term_i, term_r).astype(BF)
        keep[rows] = jnp.where(first, term_r, term_i).astype(BF)


def ahead_rows(owner, by_mode, a_ref, z_s, tgt, out):
    def gather(ref, part, first_q):
        starts = [pl.multiple_of(32 * (first_q + k) + 16 * owner, 16) for k in range(8)]
        return jnp.concatenate([ref[part, pl.ds(start, 16)] for start in starts], 0)

    for first_q in (0, 8):
        kr = gather(a_ref, 0, first_q)
        ki = gather(a_ref, 1, first_q)
        ahead_r = dot(kr, z_s[0]) - dot(ki, z_s[1])
        ahead_i = dot(kr, z_s[1]) + dot(ki, z_s[0])
        br = gather(tgt, 0, first_q).astype(F32)
        bi = gather(tgt, 1, first_q).astype(F32)
        terms = (br * ahead_r + bi * ahead_i, bi * ahead_r - br * ahead_i)
        for low in range(8):
            q = first_q + low
            for w in range(16):
                part, half, col = w // 8, w // 4 % 2, w % 4
                top = low * 16 + half * 8
                tile = terms[part][top : top + 8, col * 128 : (col + 1) * 128]
                out[jnp.where(by_mode, q, w), jnp.where(by_mode, w, q)] = tile.astype(out.dtype)


def ahead_kernel(core_ref, mode_ref, own, other, a_ref, tgt, fld, mask_out, z_s, send, mask):
    first = core_ref[0] == 0
    total = jnp.zeros((CHUNK, N), F32)
    for r in range(N // CHUNK):
        a = own[r].astype(F32)
        b = other[r].astype(F32)
        total = total + (a * a + b * b)
    bias = jnp.sum(total) / (N * N) + 1e-06
    for r in range(0, N, BLK):
        rows = slice(r, r + BLK)
        a = own[r // CHUNK : (r + BLK) // CHUNK].reshape(BLK, N).astype(F32)
        b = other[r // CHUNK : (r + BLK) // CHUNK].reshape(BLK, N).astype(F32)
        factor = lax.rsqrt(a * a + b * b + bias)
        a = a * factor
        b = b * factor
        mr = jnp.where(first, a, b).astype(BF)
        mi = jnp.where(first, b, a).astype(BF)
        mask[0, rows] = mr
        mask[1, rows] = mi
        mr = mr.astype(F32)
        mi = mi.astype(F32)
        fr = fld[0, rows].astype(F32)
        fi = fld[1, rows].astype(F32)
        gr = (fr * mr - fi * mi).astype(BF)
        gi = (fr * mi + fi * mr).astype(BF)
        z_s[0, rows] = (dot(gr, a_ref[0]) - dot(gi, a_ref[1])).astype(BF)
        z_s[1, rows] = (dot(gi, a_ref[0]) + dot(gr, a_ref[1])).astype(BF)
    start = pl.multiple_of(mode_ref[0] * 16, 16)
    mask_out[0] = mask[0, pl.ds(start, 16)]
    mask_out[1] = mask[1, pl.ds(start, 16)]
    ahead_rows(1 - core_ref[0], core_ref[0] != 0, a_ref, z_s, tgt, send)


def keep_kernel(core_ref, a_ref, z_s, tgt, keep):
    ahead_rows(core_ref[0], core_ref[0] == 0, a_ref, z_s, tgt, keep)


def power_kernel(mode_ref, parts, tiles, message):
    total = parts[0].astype(F32)
    for k in range(1, 16):
        total = total + parts[k].astype(F32)
    tiles[...] = total
    power = jnp.broadcast_to(jnp.sum(total * total), (8, 128))
    high = power.astype(BF).astype(F32)
    row = lax.broadcasted_iota(jnp.int32, (8, 128), 0)
    power = jnp.where(row < 4, high, power - high)
    mine = jnp.concatenate([tiles[mode_ref[0] // 2], power], 0).astype(BF)
    for k in range(16):
        message[k] = mine


def phasor_kernel(core_ref, tiles, arrived, power, other, out, full):
    first = core_ref[0] == 0
    bias = jnp.sum(power[...] + other[...], 0, keepdims=True) / (4 * N * N) + 1e-06
    for half in range(2):
        for col in range(4):
            k = half * 4 + col
            a = jnp.where(first, tiles[k], arrived[k].astype(F32)[0:8])
            b = jnp.where(first, tiles[k + 8], arrived[k + 8].astype(F32)[0:8])
            factor = lax.rsqrt(a * a + b * b + bias)
            full[0, half * 8 : half * 8 + 8, col * 128 : (col + 1) * 128] = a * factor
            full[1, half * 8 : half * 8 + 8, col * 128 : (col + 1) * 128] = b * factor
    out[...] = full[...].astype(BF)


HBM = pl.BlockSpec(memory_space=pltpu.HBM)
ANY = pl.BlockSpec(memory_space=pl.ANY)
SMEM = pl.BlockSpec(memory_space=pltpu.SMEM)
VMEM = pl.BlockSpec(memory_space=pltpu.VMEM)


def call_chirp(scale, after):
    return pl.pallas_call(
        chirp_kernel,
        out_shape=jax.ShapeDtypeStruct((2, N, N), BF),
        in_specs=[SMEM, ANY],
        out_specs=VMEM,
        compiler_params=pltpu.CompilerParams(vmem_limit_bytes=8 * MIB),
        cost_estimate=pl.CostEstimate(flops=10**9, bytes_accessed=2**20, transcendentals=2**12),
        name="chirp",
    )(scale, after)


def call_back(scale, core, tgt, old, fld):
    blocks = N // STEP
    return pl.pallas_call(
        back_kernel,
        out_shape=(
            jax.ShapeDtypeStruct((N, N), BF),
            jax.ShapeDtypeStruct((N, N), BF),
        ),
        in_specs=[SMEM, SMEM, HBM, HBM, HBM],
        out_specs=(VMEM,) * 2,
        scratch_shapes=[pltpu.VMEM((2, N, N), BF)] * 6
        + [
            pltpu.SemaphoreType.DMA((3 * blocks,)),
        ],
        compiler_params=pltpu.CompilerParams(vmem_limit_bytes=52 * MIB),
        name="back_margin",
    )(scale, core, tgt, old, fld)


def call_ahead(core, mode, own, other, a, tgt, fld):
    return pl.pallas_call(
        ahead_kernel,
        out_shape=(
            jax.ShapeDtypeStruct((2, 16, N), BF),
            jax.ShapeDtypeStruct((2, N, N), BF),
            jax.ShapeDtypeStruct((16, 16, 8, 128), BF),
        ),
        in_specs=[SMEM, SMEM] + [VMEM] * 5,
        out_specs=(VMEM,) * 3,
        scratch_shapes=[pltpu.VMEM((2, N, N), BF)],
        compiler_params=pltpu.CompilerParams(vmem_limit_bytes=16 * MIB),
        name="ahead_margin",
    )(core, mode, own, other, a, tgt, fld)


def call_keep(core, a, z, tgt):
    return pl.pallas_call(
        keep_kernel,
        out_shape=jax.ShapeDtypeStruct((16, 16, 8, 128), F32),
        in_specs=[SMEM] + [VMEM] * 3,
        out_specs=VMEM,
        compiler_params=pltpu.CompilerParams(vmem_limit_bytes=16 * MIB),
        cost_estimate=pl.CostEstimate(flops=2**30, bytes_accessed=2**22, transcendentals=0),
        name="keep_margin",
    )(core, a, z, tgt)


def call_power(mode, parts):
    return pl.pallas_call(
        power_kernel,
        out_shape=(jax.ShapeDtypeStruct((16, 8, 128), F32), jax.ShapeDtypeStruct((16, 16, 128), BF)),
        in_specs=[SMEM, VMEM],
        out_specs=(VMEM, VMEM),
        compiler_params=pltpu.CompilerParams(vmem_limit_bytes=8 * MIB),
        name="tile_power",
    )(mode, parts)


def call_phasor(core, tiles, arrived, power, other):
    return pl.pallas_call(
        phasor_kernel,
        out_shape=jax.ShapeDtypeStruct((2, 16, N), BF),
        in_specs=[SMEM] + [VMEM] * 4,
        out_specs=VMEM,
        scratch_shapes=[pltpu.VMEM((2, 16, N), F32)],
        compiler_params=pltpu.CompilerParams(vmem_limit_bytes=8 * MIB),
        name="tile_phasor",
    )(core, tiles, arrived, power, other)


def device(y, xh, c, xl, z):
    return (((y * 2 + xh) * 2 + c) * 2 + xl) * 8 + z


def ring_groups(core, rows, waves):
    def groups(own, cross, c, make):
        return [[device(**make(i, j), c=c) for i in own] for j in cross]

    flat = lambda i, j: {**i, **j}
    return groups(rows, waves, core, flat) + groups(waves, rows, 1 - core, flat)


def points(**sizes):
    found = [{}]
    for name, size in sizes.items():
        found = [{**point, name: k} for point in found for k in range(size)]
    return found


def wide_groups():
    x = points(xh=2, xl=2)
    y, z = points(y=8), points(z=8)
    first = [[device(**i, **k, **j, c=0) for i in y for k in x] for j in z]
    return first + [[device(**i, **k, **j, c=1) for j in z for k in x] for i in y]


def narrow_groups():
    x = points(xh=2, xl=2)
    y, z = points(y=8), points(z=8)
    first = [[device(**i, **k, **j, c=0) for j in z] for i in y for k in x]
    return first + [[device(**i, **k, **j, c=1) for i in y] for j in z for k in x]


ROWS, WAVES = points(y=8, xh=2), points(xl=2, z=8)
RING_A = ring_groups(0, ROWS, WAVES)
RING_B = ring_groups(1, ROWS, WAVES)
WIDE = wide_groups()
NARROW = narrow_groups()


def exchange(x, groups):
    return lax.all_to_all(x, AXES, 0, 0, tiled=True, axis_index_groups=groups)


def spread(x, groups):
    return exchange(jnp.broadcast_to(x[None], (len(groups[0]),) + x.shape), groups)


def total_of(x):
    return jnp.sum(x.astype(F32), 0).astype(BF)


def swap_cores(x):
    return lax.ppermute(x, "c", [(0, 1), (1, 0)])


def local(field_in, target, mask_old, scales):
    fld = field_in[0, 0]
    tgt = target[0, 0]
    core = lax.axis_index("c").reshape(1)
    mode = lax.axis_index(MODE).reshape(1)
    keep, send = call_back(scales, core, tgt, mask_old, fld)
    half = (keep.astype(F32) + swap_cores(send).astype(F32)).astype(BF)
    part = total_of(exchange(half.reshape(N // CHUNK, CHUNK, N), WIDE))
    part = total_of(spread(part, NARROW))
    own = spread(part, WIDE)
    other = swap_cores(own)
    a = call_chirp(scales, own)
    mask_one, middle, send = call_ahead(core, mode, own, other, a, tgt, fld)
    came = swap_cores(send)
    keep = call_keep(core, a, middle, tgt)
    half = (keep + came.astype(F32)).astype(BF)
    part = total_of(exchange(half, RING_A))
    tiles, message = call_power(mode, spread(part, RING_B))
    arrived = exchange(message, RING_A)
    power = jnp.sum(arrived[:, 8:].astype(F32), 0)
    return mask_one, call_phasor(core, tiles, arrived, power, swap_cores(power))


def solution(mesh):
    fine = Mesh(mesh.devices.reshape(SIZES), AXES)
    data = P(WAVE, MODE, None, None, None)
    rows = P(None, MODE, None)
    return jax.shard_map(
        local,
        mesh=fine,
        in_specs=(data, data, P(), P(WAVE)),
        out_specs=(rows, rows),
        check_vma=False,
    )
```

```python
import jax
import jax.numpy as jnp
from jax import lax
from jax.experimental import pallas as pl
from jax.experimental.pallas import tpu as pltpu
from jax.sharding import Mesh, PartitionSpec as P

N = 512
BF = jnp.bfloat16
F32 = jnp.float32
AXES = ("y", "xh", "c", "xl", "z")
SIZES = (8, 2, 2, 2, 8)
MODE = ("y", "xh", "c")
WAVE = ("xl", "z")
MIB = 1024 * 1024
BLK = 128
STEP = 256
CHUNK = 16


def dot(a, b):
    return jnp.dot(a, b, preferred_element_type=F32)


def both(left, right):
    rows = left.shape[1]
    stacked = left.reshape(2 * rows, N)
    p = dot(stacked, right[0])
    q = dot(stacked, right[1])
    return p[:rows], p[rows:], q[:rows], q[rows:]


def chirp_into(scale, ar, ai):
    lane = lax.broadcasted_iota(jnp.int32, (8, 2 * N), 1)
    diff = (lane - N).astype(F32)
    angle = jnp.float32(jnp.pi) * scale * diff * diff / N
    factor = jnp.float32(N) ** (-0.5)
    for ref, fn in ((ar, jnp.cos), (ai, jnp.sin)):
        line = fn(angle) * factor
        for d in range(-3, 4):
            start = N + BLK * d - BLK
            window = line[0:1, start : start + 2 * BLK]
            window = jnp.broadcast_to(window, (BLK, 2 * BLK))
            rolled = pltpu.roll(window, BLK, 1, stride=1, stride_axis=0)
            block = rolled[:, :BLK].astype(BF)
            for row in range(4):
                col = row + d
                if 0 <= col < 4:
                    ref[row * BLK : (row + 1) * BLK, col * BLK : (col + 1) * BLK] = block


def chirp_kernel(scale_ref, after, a):
    chirp_into(scale_ref[0], a.at[0], a.at[1])


def back_kernel(scale_ref, core_ref, tgt_hbm, old_hbm, fld_hbm, keep, send, tgt, old, fld, a, z_s, c_s, sems):
    blocks = [slice(r, r + STEP) for r in range(0, N, STEP)]
    arrive = []
    for pairs in (((tgt_hbm, tgt), (old_hbm, old)), ((fld_hbm, fld),)):
        for rows in blocks:
            for src, dst in pairs:
                arrive.append(pltpu.make_async_copy(src.at[:, rows], dst.at[:, rows], sems.at[len(arrive)]))
    for copy in arrive:
        copy.start()
    chirp_into(scale_ref[0], a.at[0], a.at[1])
    for i, rows in enumerate(blocks):
        arrive[2 * i].wait()
        arrive[2 * i + 1].wait()
        br = tgt[0, rows].astype(F32)
        bi = tgt[1, rows].astype(F32)
        mr = old[0, rows].astype(F32)
        mi = old[1, rows].astype(F32)
        c_s[0, rows] = (br * mr + bi * mi).astype(BF)
        c_s[1, rows] = (bi * mr - br * mi).astype(BF)
        rr, ir, ri, ii = both(c_s[:, rows], a)
        z_s[0, rows] = (rr + ii).astype(BF)
        z_s[1, rows] = (ir - ri).astype(BF)
    first = core_ref[0] == 0
    for i, rows in enumerate(blocks):
        rr, ir, ri, ii = both(a[:, rows], z_s)
        back_r = rr + ii
        back_i = ri - ir
        arrive[2 * len(blocks) + i].wait()
        fr = fld[0, rows].astype(F32)
        fi = fld[1, rows].astype(F32)
        term_r = back_r * fr + back_i * fi
        term_i = back_i * fr - back_r * fi
        send[rows] = jnp.where(first, term_i, term_r).astype(BF)
        keep[rows] = jnp.where(first, term_r, term_i).astype(BF)


def ahead_rows(owner, by_mode, a_ref, z_s, tgt, out):
    def gather(ref, part, first_q):
        starts = [pl.multiple_of(32 * (first_q + k) + 16 * owner, 16) for k in range(8)]
        return jnp.concatenate([ref[part, pl.ds(start, 16)] for start in starts], 0)

    for first_q in (0, 8):
        kr = gather(a_ref, 0, first_q)
        ki = gather(a_ref, 1, first_q)
        ahead_r = dot(kr, z_s[0]) - dot(ki, z_s[1])
        ahead_i = dot(kr, z_s[1]) + dot(ki, z_s[0])
        br = gather(tgt, 0, first_q).astype(F32)
        bi = gather(tgt, 1, first_q).astype(F32)
        terms = (br * ahead_r + bi * ahead_i, bi * ahead_r - br * ahead_i)
        for low in range(8):
            q = first_q + low
            for w in range(16):
                part, half, col = w // 8, w // 4 % 2, w % 4
                top = low * 16 + half * 8
                tile = terms[part][top : top + 8, col * 128 : (col + 1) * 128]
                out[jnp.where(by_mode, q, w), jnp.where(by_mode, w, q)] = tile.astype(out.dtype)


def ahead_kernel(core_ref, mode_ref, own, other, a_ref, tgt, fld, term, mine, z_s, send):
    first = core_ref[0] == 0
    total = jnp.zeros((CHUNK, N), F32)
    for r in range(N // CHUNK):
        a = own[r].astype(F32)
        b = other[r].astype(F32)
        total = total + (a * a + b * b)
    bias = jnp.sum(total) / (N * N) + 1e-06
    for r in range(0, N, BLK):
        rows = slice(r, r + BLK)
        a = own[r // CHUNK : (r + BLK) // CHUNK].reshape(BLK, N).astype(F32)
        b = other[r // CHUNK : (r + BLK) // CHUNK].reshape(BLK, N).astype(F32)
        factor = lax.rsqrt(a * a + b * b + bias)
        a = a * factor
        b = b * factor
        mr = jnp.where(first, a, b).astype(BF)
        mi = jnp.where(first, b, a).astype(BF)
        mr = mr.astype(F32)
        mi = mi.astype(F32)
        fr = fld[0, rows].astype(F32)
        fi = fld[1, rows].astype(F32)
        gr = (fr * mr - fi * mi).astype(BF)
        gi = (fr * mi + fi * mr).astype(BF)
        z_s[0, rows] = (dot(gr, a_ref[0]) - dot(gi, a_ref[1])).astype(BF)
        z_s[1, rows] = (dot(gi, a_ref[0]) + dot(gr, a_ref[1])).astype(BF)
    term[...] = jnp.full((8, 128), bias, F32)
    mine[0] = own[mode_ref[0]]
    mine[1] = other[mode_ref[0]]
    ahead_rows(1 - core_ref[0], core_ref[0] != 0, a_ref, z_s, tgt, send)


def keep_kernel(core_ref, a_ref, z_s, tgt, keep):
    ahead_rows(core_ref[0], core_ref[0] == 0, a_ref, z_s, tgt, keep)


def power_kernel(mode_ref, parts, tiles, message):
    total = parts[0].astype(F32)
    for k in range(1, 16):
        total = total + parts[k].astype(F32)
    tiles[...] = total
    power = jnp.broadcast_to(jnp.sum(total * total), (8, 128))
    high = power.astype(BF).astype(F32)
    row = lax.broadcasted_iota(jnp.int32, (8, 128), 0)
    power = jnp.where(row < 4, high, power - high)
    mine = jnp.concatenate([tiles[mode_ref[0] // 2], power], 0).astype(BF)
    for k in range(16):
        message[k] = mine


def phasor_kernel(core_ref, tiles, arrived, power, other, mine, term, mask_one, out, full):
    first = core_ref[0] == 0
    a = mine[0].astype(F32)
    b = mine[1].astype(F32)
    factor = lax.rsqrt(a * a + b * b + term[:1, :1])
    a = a * factor
    b = b * factor
    mask_one[0] = jnp.where(first, a, b).astype(BF)
    mask_one[1] = jnp.where(first, b, a).astype(BF)
    bias = jnp.sum(power[...] + other[...], 0, keepdims=True) / (4 * N * N) + 1e-06
    for half in range(2):
        for col in range(4):
            k = half * 4 + col
            a = jnp.where(first, tiles[k], arrived[k].astype(F32)[0:8])
            b = jnp.where(first, tiles[k + 8], arrived[k + 8].astype(F32)[0:8])
            factor = lax.rsqrt(a * a + b * b + bias)
            full[0, half * 8 : half * 8 + 8, col * 128 : (col + 1) * 128] = a * factor
            full[1, half * 8 : half * 8 + 8, col * 128 : (col + 1) * 128] = b * factor
    out[...] = full[...].astype(BF)


HBM = pl.BlockSpec(memory_space=pltpu.HBM)
ANY = pl.BlockSpec(memory_space=pl.ANY)
SMEM = pl.BlockSpec(memory_space=pltpu.SMEM)
VMEM = pl.BlockSpec(memory_space=pltpu.VMEM)


def call_chirp(scale, after):
    return pl.pallas_call(
        chirp_kernel,
        out_shape=jax.ShapeDtypeStruct((2, N, N), BF),
        in_specs=[SMEM, ANY],
        out_specs=VMEM,
        compiler_params=pltpu.CompilerParams(vmem_limit_bytes=8 * MIB),
        cost_estimate=pl.CostEstimate(flops=10**9, bytes_accessed=2**20, transcendentals=2**12),
        name="chirp",
    )(scale, after)


def call_back(scale, core, tgt, old, fld):
    blocks = N // STEP
    return pl.pallas_call(
        back_kernel,
        out_shape=(
            jax.ShapeDtypeStruct((N, N), BF),
            jax.ShapeDtypeStruct((N, N), BF),
        ),
        in_specs=[SMEM, SMEM, HBM, HBM, HBM],
        out_specs=(VMEM,) * 2,
        scratch_shapes=[pltpu.VMEM((2, N, N), BF)] * 6
        + [
            pltpu.SemaphoreType.DMA((3 * blocks,)),
        ],
        compiler_params=pltpu.CompilerParams(vmem_limit_bytes=52 * MIB),
        name="back_margin",
    )(scale, core, tgt, old, fld)


def call_ahead(core, mode, own, other, a, tgt, fld):
    return pl.pallas_call(
        ahead_kernel,
        out_shape=(
            jax.ShapeDtypeStruct((8, 128), F32),
            jax.ShapeDtypeStruct((2, CHUNK, N), BF),
            jax.ShapeDtypeStruct((2, N, N), BF),
            jax.ShapeDtypeStruct((16, 16, 8, 128), BF),
        ),
        in_specs=[SMEM, SMEM] + [VMEM] * 5,
        out_specs=(VMEM,) * 4,
        compiler_params=pltpu.CompilerParams(vmem_limit_bytes=16 * MIB),
        name="ahead_margin",
    )(core, mode, own, other, a, tgt, fld)


def call_keep(core, a, z, tgt):
    return pl.pallas_call(
        keep_kernel,
        out_shape=jax.ShapeDtypeStruct((16, 16, 8, 128), F32),
        in_specs=[SMEM] + [VMEM] * 3,
        out_specs=VMEM,
        compiler_params=pltpu.CompilerParams(vmem_limit_bytes=16 * MIB),
        cost_estimate=pl.CostEstimate(flops=2**30, bytes_accessed=2**22, transcendentals=0),
        name="keep_margin",
    )(core, a, z, tgt)


def call_power(mode, parts):
    return pl.pallas_call(
        power_kernel,
        out_shape=(jax.ShapeDtypeStruct((16, 8, 128), F32), jax.ShapeDtypeStruct((16, 16, 128), BF)),
        in_specs=[SMEM, VMEM],
        out_specs=(VMEM, VMEM),
        compiler_params=pltpu.CompilerParams(vmem_limit_bytes=8 * MIB),
        name="tile_power",
    )(mode, parts)


def call_phasor(core, *arrays):
    return pl.pallas_call(
        phasor_kernel,
        out_shape=(jax.ShapeDtypeStruct((2, 16, N), BF),) * 2,
        in_specs=[SMEM] + [VMEM] * 6,
        out_specs=(VMEM, VMEM),
        scratch_shapes=[pltpu.VMEM((2, 16, N), F32)],
        compiler_params=pltpu.CompilerParams(vmem_limit_bytes=8 * MIB),
        name="tile_phasor",
    )(core, *arrays)


def device(y, xh, c, xl, z):
    return (((y * 2 + xh) * 2 + c) * 2 + xl) * 8 + z


def ring_groups(core, rows, waves):
    def groups(own, cross, c, make):
        return [[device(**make(i, j), c=c) for i in own] for j in cross]

    flat = lambda i, j: {**i, **j}
    return groups(rows, waves, core, flat) + groups(waves, rows, 1 - core, flat)


def points(**sizes):
    found = [{}]
    for name, size in sizes.items():
        found = [{**point, name: k} for point in found for k in range(size)]
    return found


def wide_groups():
    x = points(xh=2, xl=2)
    y, z = points(y=8), points(z=8)
    first = [[device(**i, **k, **j, c=0) for i in y for k in x] for j in z]
    return first + [[device(**i, **k, **j, c=1) for j in z for k in x] for i in y]


def narrow_groups():
    x = points(xh=2, xl=2)
    y, z = points(y=8), points(z=8)
    first = [[device(**i, **k, **j, c=0) for j in z] for i in y for k in x]
    return first + [[device(**i, **k, **j, c=1) for i in y] for j in z for k in x]


ROWS, WAVES = points(y=8, xh=2), points(xl=2, z=8)
RING_A = ring_groups(0, ROWS, WAVES)
RING_B = ring_groups(1, ROWS, WAVES)
WIDE = wide_groups()
NARROW = narrow_groups()


def exchange(x, groups):
    return lax.all_to_all(x, AXES, 0, 0, tiled=True, axis_index_groups=groups)


def spread(x, groups):
    return exchange(jnp.broadcast_to(x[None], (len(groups[0]),) + x.shape), groups)


def total_of(x):
    return jnp.sum(x.astype(F32), 0).astype(BF)


def swap_cores(x):
    return lax.ppermute(x, "c", [(0, 1), (1, 0)])


def local(field_in, target, mask_old, scales):
    fld = field_in[0, 0]
    tgt = target[0, 0]
    core = lax.axis_index("c").reshape(1)
    mode = lax.axis_index(MODE).reshape(1)
    keep, send = call_back(scales, core, tgt, mask_old, fld)
    half = (keep.astype(F32) + swap_cores(send).astype(F32)).astype(BF)
    part = total_of(exchange(half.reshape(N // CHUNK, CHUNK, N), WIDE))
    part = total_of(spread(part, NARROW))
    own = spread(part, WIDE)
    other = swap_cores(own)
    a = call_chirp(scales, own)
    term, mine, middle, send = call_ahead(core, mode, own, other, a, tgt, fld)
    came = swap_cores(send)
    keep = call_keep(core, a, middle, tgt)
    half = (keep + came.astype(F32)).astype(BF)
    part = total_of(exchange(half, RING_A))
    tiles, message = call_power(mode, spread(part, RING_B))
    arrived = exchange(message, RING_A)
    power = jnp.sum(arrived[:, 8:].astype(F32), 0)
    return call_phasor(core, tiles, arrived, power, swap_cores(power), mine, term)


def solution(mesh):
    fine = Mesh(mesh.devices.reshape(SIZES), AXES)
    data = P(WAVE, MODE, None, None, None)
    rows = P(None, MODE, None)
    return jax.shard_map(
        local,
        mesh=fine,
        in_specs=(data, data, P(), P(WAVE)),
        out_specs=(rows, rows),
        check_vma=False,
    )
```

```python
import jax
import jax.numpy as jnp
from jax import lax
from jax.experimental import pallas as pl
from jax.experimental.pallas import tpu as pltpu
from jax.sharding import Mesh, PartitionSpec as P

N = 512
BF = jnp.bfloat16
F32 = jnp.float32
AXES = ("y", "xh", "c", "xl", "z")
SIZES = (8, 2, 2, 2, 8)
MODE = ("y", "xh", "c")
WAVE = ("xl", "z")
MIB = 1024 * 1024
BLK = 128
STEP = 256
CHUNK = 16


def dot(a, b):
    return jnp.dot(a, b, preferred_element_type=F32)


def both(left, right):
    rows = left.shape[1]
    stacked = left.reshape(2 * rows, N)
    p = dot(stacked, right[0])
    q = dot(stacked, right[1])
    return p[:rows], p[rows:], q[:rows], q[rows:]


def chirp_into(scale, ar, ai):
    lane = lax.broadcasted_iota(jnp.int32, (8, 2 * N), 1)
    diff = (lane - N).astype(F32)
    angle = jnp.float32(jnp.pi) * scale * diff * diff / N
    factor = jnp.float32(N) ** (-0.5)
    for ref, fn in ((ar, jnp.cos), (ai, jnp.sin)):
        line = fn(angle) * factor
        for d in range(-3, 4):
            start = N + BLK * d - BLK
            window = line[0:1, start : start + 2 * BLK]
            window = jnp.broadcast_to(window, (BLK, 2 * BLK))
            rolled = pltpu.roll(window, BLK, 1, stride=1, stride_axis=0)
            block = rolled[:, :BLK].astype(BF)
            for row in range(4):
                col = row + d
                if 0 <= col < 4:
                    ref[row * BLK : (row + 1) * BLK, col * BLK : (col + 1) * BLK] = block


def chirp_kernel(scale_ref, after, a):
    chirp_into(scale_ref[0], a.at[0], a.at[1])


def back_kernel(scale_ref, core_ref, tgt_hbm, old_hbm, fld_hbm, keep, send, tgt, old, fld, a, z_s, c_s, sems):
    blocks = [slice(r, r + STEP) for r in range(0, N, STEP)]
    arrive = []
    for pairs in (((tgt_hbm, tgt), (old_hbm, old)), ((fld_hbm, fld),)):
        for rows in blocks:
            for src, dst in pairs:
                arrive.append(pltpu.make_async_copy(src.at[:, rows], dst.at[:, rows], sems.at[len(arrive)]))
    late = 2 * len(blocks)
    for copy in arrive[:late]:
        copy.start()
    chirp_into(scale_ref[0], a.at[0], a.at[1])
    for i, rows in enumerate(blocks):
        arrive[2 * i].wait()
        arrive[2 * i + 1].wait()
        if i == 0:
            for copy in arrive[late:]:
                copy.start()
        br = tgt[0, rows].astype(F32)
        bi = tgt[1, rows].astype(F32)
        mr = old[0, rows].astype(F32)
        mi = old[1, rows].astype(F32)
        c_s[0, rows] = (br * mr + bi * mi).astype(BF)
        c_s[1, rows] = (bi * mr - br * mi).astype(BF)
        rr, ir, ri, ii = both(c_s[:, rows], a)
        z_s[0, rows] = (rr + ii).astype(BF)
        z_s[1, rows] = (ir - ri).astype(BF)
    first = core_ref[0] == 0
    rr, ir, ri, ii = both(a[...], z_s)
    back_r = rr + ii
    back_i = ri - ir
    for i, rows in enumerate(blocks):
        arrive[late + i].wait()
        fr = fld[0, rows].astype(F32)
        fi = fld[1, rows].astype(F32)
        term_r = back_r[rows] * fr + back_i[rows] * fi
        term_i = back_i[rows] * fr - back_r[rows] * fi
        send[rows] = jnp.where(first, term_i, term_r).astype(BF)
        keep[rows] = jnp.where(first, term_r, term_i).astype(BF)


def ahead_rows(owner, by_mode, a_ref, z_s, tgt, out):
    def gather(ref, part, first_q):
        starts = [pl.multiple_of(32 * (first_q + k) + 16 * owner, 16) for k in range(8)]
        return jnp.concatenate([ref[part, pl.ds(start, 16)] for start in starts], 0)

    for first_q in (0, 8):
        kr = gather(a_ref, 0, first_q)
        ki = gather(a_ref, 1, first_q)
        ahead_r = dot(kr, z_s[0]) - dot(ki, z_s[1])
        ahead_i = dot(kr, z_s[1]) + dot(ki, z_s[0])
        br = gather(tgt, 0, first_q).astype(F32)
        bi = gather(tgt, 1, first_q).astype(F32)
        terms = (br * ahead_r + bi * ahead_i, bi * ahead_r - br * ahead_i)
        for low in range(8):
            q = first_q + low
            for w in range(16):
                part, half, col = w // 8, w // 4 % 2, w % 4
                top = low * 16 + half * 8
                tile = terms[part][top : top + 8, col * 128 : (col + 1) * 128]
                out[jnp.where(by_mode, q, w), jnp.where(by_mode, w, q)] = tile.astype(out.dtype)


def ahead_kernel(core_ref, mode_ref, own, other, a_ref, tgt, fld, term, mine, z_s, send):
    first = core_ref[0] == 0
    total = jnp.zeros((CHUNK, N), F32)
    for r in range(N // CHUNK):
        a = own[r].astype(F32)
        b = other[r].astype(F32)
        total = total + (a * a + b * b)
    bias = jnp.sum(total) / (N * N) + 1e-06
    for r in range(0, N, BLK):
        rows = slice(r, r + BLK)
        a = own[r // CHUNK : (r + BLK) // CHUNK].reshape(BLK, N).astype(F32)
        b = other[r // CHUNK : (r + BLK) // CHUNK].reshape(BLK, N).astype(F32)
        factor = lax.rsqrt(a * a + b * b + bias)
        a = a * factor
        b = b * factor
        mr = jnp.where(first, a, b).astype(BF)
        mi = jnp.where(first, b, a).astype(BF)
        mr = mr.astype(F32)
        mi = mi.astype(F32)
        fr = fld[0, rows].astype(F32)
        fi = fld[1, rows].astype(F32)
        gr = (fr * mr - fi * mi).astype(BF)
        gi = (fr * mi + fi * mr).astype(BF)
        z_s[0, rows] = (dot(gr, a_ref[0]) - dot(gi, a_ref[1])).astype(BF)
        z_s[1, rows] = (dot(gi, a_ref[0]) + dot(gr, a_ref[1])).astype(BF)
    term[...] = jnp.full((8, 128), bias, F32)
    mine[0] = own[mode_ref[0]]
    mine[1] = other[mode_ref[0]]
    ahead_rows(1 - core_ref[0], core_ref[0] != 0, a_ref, z_s, tgt, send)


def keep_kernel(core_ref, a_ref, z_s, tgt, keep):
    ahead_rows(core_ref[0], core_ref[0] == 0, a_ref, z_s, tgt, keep)


def power_kernel(mode_ref, parts, tiles, message):
    total = parts[0].astype(F32)
    for k in range(1, 16):
        total = total + parts[k].astype(F32)
    tiles[...] = total
    power = jnp.broadcast_to(jnp.sum(total * total), (8, 128))
    high = power.astype(BF).astype(F32)
    row = lax.broadcasted_iota(jnp.int32, (8, 128), 0)
    power = jnp.where(row < 4, high, power - high)
    mine = jnp.concatenate([tiles[mode_ref[0] // 2], power], 0).astype(BF)
    for k in range(16):
        message[k] = mine


def phasor_kernel(core_ref, tiles, arrived, power, other, mine, term, mask_one, out, full):
    first = core_ref[0] == 0
    a = mine[0].astype(F32)
    b = mine[1].astype(F32)
    factor = lax.rsqrt(a * a + b * b + term[:1, :1])
    a = a * factor
    b = b * factor
    mask_one[0] = jnp.where(first, a, b).astype(BF)
    mask_one[1] = jnp.where(first, b, a).astype(BF)
    bias = jnp.sum(power[...] + other[...], 0, keepdims=True) / (4 * N * N) + 1e-06
    for half in range(2):
        for col in range(4):
            k = half * 4 + col
            a = jnp.where(first, tiles[k], arrived[k].astype(F32)[0:8])
            b = jnp.where(first, tiles[k + 8], arrived[k + 8].astype(F32)[0:8])
            factor = lax.rsqrt(a * a + b * b + bias)
            full[0, half * 8 : half * 8 + 8, col * 128 : (col + 1) * 128] = a * factor
            full[1, half * 8 : half * 8 + 8, col * 128 : (col + 1) * 128] = b * factor
    out[...] = full[...].astype(BF)


HBM = pl.BlockSpec(memory_space=pltpu.HBM)
ANY = pl.BlockSpec(memory_space=pl.ANY)
SMEM = pl.BlockSpec(memory_space=pltpu.SMEM)
VMEM = pl.BlockSpec(memory_space=pltpu.VMEM)


def call_chirp(scale, after):
    return pl.pallas_call(
        chirp_kernel,
        out_shape=jax.ShapeDtypeStruct((2, N, N), BF),
        in_specs=[SMEM, ANY],
        out_specs=VMEM,
        compiler_params=pltpu.CompilerParams(vmem_limit_bytes=8 * MIB),
        cost_estimate=pl.CostEstimate(flops=10**9, bytes_accessed=2**20, transcendentals=2**12),
        name="chirp",
    )(scale, after)


def call_back(scale, core, tgt, old, fld):
    blocks = N // STEP
    return pl.pallas_call(
        back_kernel,
        out_shape=(
            jax.ShapeDtypeStruct((N, N), BF),
            jax.ShapeDtypeStruct((N, N), BF),
        ),
        in_specs=[SMEM, SMEM, HBM, HBM, HBM],
        out_specs=(VMEM,) * 2,
        scratch_shapes=[pltpu.VMEM((2, N, N), BF)] * 6
        + [
            pltpu.SemaphoreType.DMA((3 * blocks,)),
        ],
        compiler_params=pltpu.CompilerParams(vmem_limit_bytes=52 * MIB),
        name="back_margin",
    )(scale, core, tgt, old, fld)


def call_ahead(core, mode, own, other, a, tgt, fld):
    return pl.pallas_call(
        ahead_kernel,
        out_shape=(
            jax.ShapeDtypeStruct((8, 128), F32),
            jax.ShapeDtypeStruct((2, CHUNK, N), BF),
            jax.ShapeDtypeStruct((2, N, N), BF),
            jax.ShapeDtypeStruct((16, 16, 8, 128), BF),
        ),
        in_specs=[SMEM, SMEM] + [VMEM] * 5,
        out_specs=(VMEM,) * 4,
        compiler_params=pltpu.CompilerParams(vmem_limit_bytes=16 * MIB),
        name="ahead_margin",
    )(core, mode, own, other, a, tgt, fld)


def call_keep(core, a, z, tgt):
    return pl.pallas_call(
        keep_kernel,
        out_shape=jax.ShapeDtypeStruct((16, 16, 8, 128), F32),
        in_specs=[SMEM] + [VMEM] * 3,
        out_specs=VMEM,
        compiler_params=pltpu.CompilerParams(vmem_limit_bytes=16 * MIB),
        cost_estimate=pl.CostEstimate(flops=2**30, bytes_accessed=2**22, transcendentals=0),
        name="keep_margin",
    )(core, a, z, tgt)


def call_power(mode, parts):
    return pl.pallas_call(
        power_kernel,
        out_shape=(jax.ShapeDtypeStruct((16, 8, 128), F32), jax.ShapeDtypeStruct((16, 16, 128), BF)),
        in_specs=[SMEM, VMEM],
        out_specs=(VMEM, VMEM),
        compiler_params=pltpu.CompilerParams(vmem_limit_bytes=8 * MIB),
        name="tile_power",
    )(mode, parts)


def call_phasor(core, *arrays):
    return pl.pallas_call(
        phasor_kernel,
        out_shape=(jax.ShapeDtypeStruct((2, 16, N), BF),) * 2,
        in_specs=[SMEM] + [VMEM] * 6,
        out_specs=(VMEM, VMEM),
        scratch_shapes=[pltpu.VMEM((2, 16, N), F32)],
        compiler_params=pltpu.CompilerParams(vmem_limit_bytes=8 * MIB),
        name="tile_phasor",
    )(core, *arrays)


def device(y, xh, c, xl, z):
    return (((y * 2 + xh) * 2 + c) * 2 + xl) * 8 + z


def ring_groups(core, rows, waves):
    def groups(own, cross, c, make):
        return [[device(**make(i, j), c=c) for i in own] for j in cross]

    flat = lambda i, j: {**i, **j}
    return groups(rows, waves, core, flat) + groups(waves, rows, 1 - core, flat)


def points(**sizes):
    found = [{}]
    for name, size in sizes.items():
        found = [{**point, name: k} for point in found for k in range(size)]
    return found


def wide_groups():
    x = points(xh=2, xl=2)
    y, z = points(y=8), points(z=8)
    first = [[device(**i, **k, **j, c=0) for i in y for k in x] for j in z]
    return first + [[device(**i, **k, **j, c=1) for j in z for k in x] for i in y]


def narrow_groups():
    x = points(xh=2, xl=2)
    y, z = points(y=8), points(z=8)
    first = [[device(**i, **k, **j, c=0) for j in z] for i in y for k in x]
    return first + [[device(**i, **k, **j, c=1) for i in y] for j in z for k in x]


ROWS, WAVES = points(y=8, xh=2), points(xl=2, z=8)
RING_A = ring_groups(0, ROWS, WAVES)
RING_B = ring_groups(1, ROWS, WAVES)
WIDE = wide_groups()
NARROW = narrow_groups()


def exchange(x, groups):
    return lax.all_to_all(x, AXES, 0, 0, tiled=True, axis_index_groups=groups)


def spread(x, groups):
    return exchange(jnp.broadcast_to(x[None], (len(groups[0]),) + x.shape), groups)


def total_of(x):
    return jnp.sum(x.astype(F32), 0).astype(BF)


def swap_cores(x):
    return lax.ppermute(x, "c", [(0, 1), (1, 0)])


def local(field_in, target, mask_old, scales):
    fld = field_in[0, 0]
    tgt = target[0, 0]
    core = lax.axis_index("c").reshape(1)
    mode = lax.axis_index(MODE).reshape(1)
    keep, send = call_back(scales, core, tgt, mask_old, fld)
    half = (keep.astype(F32) + swap_cores(send).astype(F32)).astype(BF)
    part = total_of(exchange(half.reshape(N // CHUNK, CHUNK, N), WIDE))
    part = total_of(spread(part, NARROW))
    own = spread(part, WIDE)
    other = swap_cores(own)
    a = call_chirp(scales, own)
    term, mine, middle, send = call_ahead(core, mode, own, other, a, tgt, fld)
    came = swap_cores(send)
    keep = call_keep(core, a, middle, tgt)
    half = (keep + came.astype(F32)).astype(BF)
    part = total_of(exchange(half, RING_A))
    tiles, message = call_power(mode, spread(part, RING_B))
    arrived = exchange(message, RING_A)
    power = jnp.sum(arrived[:, 8:].astype(F32), 0)
    return call_phasor(core, tiles, arrived, power, swap_cores(power), mine, term)


def solution(mesh):
    fine = Mesh(mesh.devices.reshape(SIZES), AXES)
    data = P(WAVE, MODE, None, None, None)
    rows = P(None, MODE, None)
    return jax.shard_map(
        local,
        mesh=fine,
        in_specs=(data, data, P(), P(WAVE)),
        out_specs=(rows, rows),
        check_vma=False,
    )
```
